32 devices in a mesh: row: 4 (over y, core), col: 8 (over z, x).
Axes of the slice: x: 2, y: 2, z: 4, core: 2. Of those that a mesh axis runs over, the one named last changes fastest.
Arguments:
- blocks: bfloat16 [256, 16, 512, 512], P('row', 'col'), may hold values from 3.8146973e-06 to 0.32348633, as said below
- source_ids: int32 [256, 16], P('row', 'col'), may hold values from 0 to 255, as said below
- emission: bfloat16 [5008, 131072], P('col', 'row'), may hold values from 0.05 to 5120, as said below
- tokens: int32 [4, 104], replicated, may hold values from 0 to 5007, as said below
Outputs:
- posterior: bfloat16 [104, 131072], P(None, ('row', 'col'))
- log_total: float32 [104], replicated
The draws below stay inside these ranges and needn't reach their ends.
Inputs may be any that keep to these rules, and one draw needn't show every extreme that they name: Block id source_ids[J, k] lies in the group g of 8 consecutive blocks (g = id // 8) with g % 8 == k // (16 // 8). In every step exactly 26 of the 104 tokens lie in one range of 5008 // 8 consecutive ids, which one is drawn, and no such range holds more. `emission`: positive weights. `blocks`: positive weights.
All inputs are finite; a program needn't handle non-finite values.
Results may differ from the reference program's by a relative error of at most 0.029.
Values may be sent and summed in bfloat16 or wider, within the bound.
No kernel may reach another device: no remote copies, remote signals or barrier semaphores. Data moves between devices by JAX's collectives and lax.ppermute only.
A program may use at most 256 MiB of HBM per device.

```python
import math
import jax
import jax.numpy as jnp
from jax import lax

STATES = 131072
BLOCK = 512
SLOTS = 16
VOCAB = 5008
STEPS = 3
SEQS = 104
CAP = 26
NB = 256
PIECE_BLOCKS = 8
N_ROW = 4
N_COL = 8


def draw_blocks(key, part):
    key = jax.random.fold_in(key, 14)
    value_key, slot_key = jax.random.split(key)
    cutoff = 0.97
    height = 200.0
    uniform_values = jax.random.uniform(value_key, (NB, SLOTS, BLOCK, BLOCK), jnp.float32)
    peaks = jnp.maximum(uniform_values - cutoff, 0.0) * (height / (1.0 - cutoff))
    diagonal = 4.0 * BLOCK * jnp.eye(BLOCK, dtype=jnp.float32)
    slot_scale = jnp.exp(jax.random.uniform(slot_key, (NB, SLOTS, 1, 1), jnp.float32, 0.0, math.log(32.0)))
    values = 1.0 + uniform_values + peaks + diagonal[None, None, :, :]
    return (values * slot_scale / (32.0 * SLOTS * BLOCK)).astype(jnp.bfloat16)


def draw_emission(key, part):
    key = jax.random.fold_in(key, 11)
    value_key, row_key, within_key = jax.random.split(key, 3)
    position = jnp.arange(STATES, dtype=jnp.float32) / STATES
    within_pattern = jnp.exp(jax.random.uniform(within_key, (VOCAB, 1, BLOCK), jnp.float32, 0.0, math.log(10.0)))
    raw_values = jnp.exp(jax.random.uniform(value_key, (VOCAB, STATES), jnp.float32, math.log(0.05), 0.0))
    row_scale = jnp.exp(jax.random.uniform(row_key, (VOCAB, 1), jnp.float32, 0.0, math.log(10.0)))
    state_scale = jnp.power(10.0, position)
    values = (raw_values * row_scale * state_scale[None, :]).reshape(VOCAB, NB, BLOCK) * within_pattern
    return values.reshape(VOCAB, STATES).astype(jnp.bfloat16)


def draw_source_ids(key, part):
    key = jax.random.fold_in(key, 12)
    row_key, within_key = jax.random.split(key)
    slots_col = SLOTS // N_COL
    group_col = jnp.arange(SLOTS, dtype=jnp.int32) // slots_col
    row_pick = jax.random.randint(row_key, (NB, SLOTS), 0, N_ROW, dtype=jnp.int32)
    within = jax.random.randint(within_key, (NB, SLOTS), 0, PIECE_BLOCKS, dtype=jnp.int32)
    return ((row_pick * N_COL + group_col[None, :]) * PIECE_BLOCKS + within).astype(jnp.int32)


def draw_tokens(key, part):
    key = jax.random.fold_in(key, 13)
    vocab_col = VOCAB // N_COL

    def single_step(step_key):
        busy_key, order_key, inner_key = jax.random.split(step_key, 3)
        busiest = jax.random.randint(busy_key, (), 0, N_COL, dtype=jnp.int32)
        position = jnp.arange(SEQS, dtype=jnp.int32)
        offset = jnp.where(position < CAP, 0, 1 + (position - CAP) % (N_COL - 1))
        owner = jax.random.permutation(order_key, (busiest + offset) % N_COL)
        inner = jax.random.randint(inner_key, (SEQS,), 0, vocab_col, dtype=jnp.int32)
        return owner * vocab_col + inner
    return jax.vmap(single_step)(jax.random.split(key, STEPS + 1)).astype(jnp.int32)


def setup_inputs(seed: int = 0) -> dict:
    splits = jax.random.split(jax.random.key(seed), 5)
    return {
        "blocks": draw_blocks(jax.random.fold_in(splits[4], 71), 0),
        "source_ids": draw_source_ids(jax.random.fold_in(splits[4], 71), 0),
        "emission": draw_emission(jax.random.fold_in(splits[4], 71), 0),
        "tokens": draw_tokens(jax.random.fold_in(splits[4], 71), 0),
    }


def reference(blocks, source_ids, emission, tokens):
    block_count = STATES // BLOCK
    slots_col = SLOTS // N_COL

    def normalize(weighted):
        scale = jnp.sum(weighted, axis=1) / STATES
        return (weighted / scale[:, None]).astype(jnp.bfloat16), jnp.log(scale)

    def transition(states_now):
        split_states = states_now.reshape(SEQS, block_count, BLOCK)

        def block_row(record):
            block_vals, source_list = record
            sources = jnp.take(split_states, source_list, axis=1).astype(jnp.float32)
            terms = jnp.einsum("bkm,kmn->kbn", sources, block_vals.astype(jnp.float32))
            grouped = jnp.sum(terms.reshape(N_COL, slots_col, SEQS, BLOCK), axis=1)
            rounded = lax.optimization_barrier(grouped.astype(jnp.bfloat16))
            return jnp.sum(rounded.astype(jnp.float32), axis=0)

        carried = lax.map(block_row, (blocks, source_ids))
        return jnp.transpose(carried, (1, 0, 2)).reshape(SEQS, STATES)

    weighted = emission[tokens[0]].astype(jnp.float32)
    states_now, log_total = normalize(weighted)
    for position in range(1, STEPS + 1):
        weighted = emission[tokens[position]].astype(jnp.float32) * transition(states_now)
        states_now, log_part = normalize(weighted)
        log_total = log_total + log_part
    return states_now, log_total
```

```python
import functools

import jax
import jax.numpy as jnp
from jax import lax
from jax.experimental import pallas as pl
from jax.experimental.pallas import tpu as pltpu
from jax.sharding import PartitionSpec as P

CAP = 26
CAP_PAD = 32
FOLD = 4


def ring_order(count):
    return list(range(0, count, 2)) + list(range(count - 1 - count % 2, 0, -2))


def pick_kernel(spans, ids_ref, table_ref, *refs):
    out_refs, staged = refs[:-1], refs[-1]
    rows = ids_ref.shape[0]
    vocab = table_ref.shape[0]
    wanted = lax.broadcasted_iota(jnp.int32, (rows, vocab), 1) == ids_ref[...]
    onehot = jnp.where(wanted, 1.0, 0.0).astype(jnp.bfloat16)
    value = jnp.dot(onehot, table_ref[...], preferred_element_type=jnp.float32)
    lanes = value.shape[1] // FOLD
    for low, out_ref in zip(spans, out_refs):
        for fold in range(FOLD):
            staged[fold * CAP : (fold + 1) * CAP, :] = value[
                low : low + CAP, fold * lanes : (fold + 1) * lanes
            ]
        out_ref[0] = staged[...].astype(out_ref.dtype)


def pick(ids, table, pieces):
    vocab, panel = table.shape
    steps, padded = ids.shape
    width = panel // pieces
    lanes = width // FOLD
    return pl.pallas_call(
        functools.partial(pick_kernel, [t * padded for t in range(steps)]),
        grid=(pieces,),
        in_specs=[
            pl.BlockSpec((steps * padded, 1), lambda i: (0, 0)),
            pl.BlockSpec((vocab, width), lambda i: (0, i)),
        ],
        out_specs=[pl.BlockSpec((1, FOLD * CAP, lanes), lambda i: (i, 0, 0))] * steps,
        out_shape=[jax.ShapeDtypeStruct((pieces, FOLD * CAP, lanes), table.dtype)] * steps,
        scratch_shapes=[pltpu.VMEM((FOLD * CAP, lanes), jnp.float32)],
        cost_estimate=pl.CostEstimate(
            flops=2 * steps * padded * vocab * width * pieces,
            bytes_accessed=2 * pieces * width * (vocab + steps * CAP),
            transcendentals=0,
        ),
        compiler_params=pltpu.CompilerParams(vmem_limit_bytes=40 << 20),
        name="pick",
    )(ids.reshape(-1, 1), table)


def fold_kernel(rows_ref, *out_refs):
    *out_refs, staged = out_refs
    lanes = staged.shape[1]
    for share, out_ref in enumerate(out_refs):
        for fold in range(FOLD):
            low = (share * FOLD + fold) * lanes
            staged[fold * CAP : (fold + 1) * CAP, :] = rows_ref[
                :CAP, low : low + lanes
            ].astype(jnp.float32)
        out_ref[0] = staged[...].astype(out_ref.dtype)


def fold_rows(rows, pieces, shares):
    padded, panel = rows.shape
    lanes = panel // pieces // shares // FOLD
    return pl.pallas_call(
        fold_kernel,
        grid=(pieces,),
        in_specs=[pl.BlockSpec((padded, panel // pieces), lambda i: (0, i))],
        out_specs=[pl.BlockSpec((1, FOLD * CAP, lanes), lambda i: (i, 0, 0))] * shares,
        out_shape=[jax.ShapeDtypeStruct((pieces, FOLD * CAP, lanes), rows.dtype)] * shares,
        scratch_shapes=[pltpu.VMEM((FOLD * CAP, lanes), jnp.float32)],
        cost_estimate=pl.CostEstimate(
            flops=0, bytes_accessed=4 * padded * panel, transcendentals=0
        ),
        compiler_params=pltpu.CompilerParams(vmem_limit_bytes=40 << 20),
        name="fold_rows",
    )(rows)


def place_kernel(index_ref, table_ref, out_ref):
    seqs = index_ref.shape[0]
    height = table_ref.shape[0]
    index = index_ref[...] + pl.program_id(0) * CAP
    wanted = lax.broadcasted_iota(jnp.int32, (seqs, height), 1) == index
    onehot = jnp.where(wanted, 1.0, 0.0).astype(jnp.bfloat16)
    out_ref[...] = jnp.dot(
        onehot, table_ref[...], preferred_element_type=jnp.float32
    ).astype(out_ref.dtype)


def place(index, messages):
    pieces, rows, lanes = messages.shape
    seqs = index.shape[0]
    return pl.pallas_call(
        place_kernel,
        grid=(FOLD,),
        in_specs=[
            pl.BlockSpec((seqs, 1), lambda i: (0, 0)),
            pl.BlockSpec((pieces * rows, lanes), lambda i: (0, 0)),
        ],
        out_specs=pl.BlockSpec((seqs, lanes), lambda i: (0, i)),
        out_shape=jax.ShapeDtypeStruct((seqs, FOLD * lanes), messages.dtype),
        cost_estimate=pl.CostEstimate(
            flops=2 * FOLD * seqs * pieces * rows * lanes,
            bytes_accessed=2 * lanes * (pieces * rows + FOLD * seqs),
            transcendentals=0,
        ),
        compiler_params=pltpu.CompilerParams(vmem_limit_bytes=40 << 20),
        name="place",
    )(index.reshape(-1, 1), messages.reshape(pieces * rows, lanes))


def partial_kernel(parts, chunk_ref, code_ref, *refs):
    part_refs, (blocks_ref, *out_refs, held, sems) = refs[:parts], refs[parts:]
    step = pl.program_id(0)
    half, slots, width, _ = blocks_ref.shape
    piece_blocks = held.shape[2] // width

    @pl.when(step == 0)
    def _load():
        copies = []
        for number, part_ref in enumerate(part_refs):
            columns = part_ref.shape[1]
            copies.append(
                pltpu.make_async_copy(
                    part_ref,
                    held.at[number // 2, :, pl.ds(number % 2 * columns, columns)],
                    sems.at[number],
                )
            )
        for copy in copies:
            copy.start()
        for copy in copies:
            copy.wait()

    totals = []
    for block in range(half):
        total = None
        for slot in range(slots):
            code = code_ref[(chunk_ref[step] * half + block) * slots + slot]
            start = pl.multiple_of(code % piece_blocks * width, width)
            source = held[code // piece_blocks, :, pl.ds(start, width)]
            term = jnp.dot(
                source, blocks_ref[block, slot], preferred_element_type=jnp.float32
            )
            total = term if total is None else total + term
        totals.append(total)

    for number, out_ref in enumerate(out_refs):

        @pl.when(step == number)
        def _store(out_ref=out_ref):
            for block, total in enumerate(totals):
                out_ref[:, block * width : (block + 1) * width] = total


def partial_sums(chunk, code, parts, blocks, half):
    _, slots, width, _ = blocks.shape
    seqs, columns = parts[0].shape
    count = len(parts)
    return pl.pallas_call(
        functools.partial(partial_kernel, count),
        grid_spec=pltpu.PrefetchScalarGridSpec(
            num_scalar_prefetch=2,
            grid=(2,),
            in_specs=[pl.BlockSpec(memory_space=pl.ANY)] * count
            + [
                pl.BlockSpec(
                    (half, slots, width, width),
                    lambda i, chunk, code: (chunk[i], 0, 0, 0),
                )
            ],
            out_specs=[pl.BlockSpec((seqs, columns), lambda i, chunk, code: (0, 0))] * 2,
            scratch_shapes=[
                pltpu.VMEM((count // 2, seqs, 2 * columns), jnp.bfloat16),
                pltpu.SemaphoreType.DMA((count,)),
            ],
        ),
        out_shape=[jax.ShapeDtypeStruct((seqs, columns), jnp.float32)] * 2,
        cost_estimate=pl.CostEstimate(
            flops=4 * half * slots * seqs * width * width,
            bytes_accessed=4 * half * slots * width * width + 2 * count * seqs * columns,
            transcendentals=0,
        ),
        compiler_params=pltpu.CompilerParams(vmem_limit_bytes=40 << 20),
        name="partial_sums",
    )(chunk, code, *parts, blocks)


def on_device(blocks, source_ids, emission, tokens):
    row_count = lax.axis_size("row")
    col_count = lax.axis_size("col")
    row_index = lax.axis_index("row")
    col_index = lax.axis_index("col")
    local_rows, local_slots, width, _ = blocks.shape
    vocab_local, panel = emission.shape
    piece = panel // col_count
    piece_blocks = piece // width
    half = piece_blocks // 2
    total_steps, seq_count = tokens.shape
    states = panel * row_count

    owner = tokens // vocab_local
    inner = tokens % vocab_local
    same = owner[:, :, None] == owner[:, None, :]
    earlier = jnp.arange(seq_count)[:, None] > jnp.arange(seq_count)[None, :]
    rank = jnp.sum((same & earlier[None]).astype(jnp.int32), axis=2)
    mine = (owner == col_index)[:, None, :] & (
        rank[:, None, :] == jnp.arange(CAP_PAD)[None, :, None]
    )
    ids = jnp.sum(jnp.where(mine, inner[:, None, :], 0), axis=2)
    index = owner * (FOLD * CAP) + rank

    def exchange(values):
        return lax.all_to_all(values, "col", 0, 0, tiled=True)

    first = jnp.take(emission, ids[0], axis=0, mode="clip")
    now = [place(index[0], exchange(sent)) for sent in fold_rows(first, col_count, 2)]
    later = pick(ids[1:], emission, col_count)

    group = source_ids // piece_blocks
    code = ((group // col_count) ^ row_index) * piece_blocks + source_ids % piece_blocks
    code = code.reshape(-1).astype(jnp.int32)

    order = ring_order(col_count)
    position = jnp.array([order.index(c) for c in range(col_count)], jnp.int32)[col_index]
    order_table = jnp.array(order, jnp.int32)
    hops = jnp.arange(col_count, dtype=jnp.int32)
    up = order_table[(position - 1 - hops) % col_count]
    down = order_table[(position + 1 + hops) % col_count]
    chunks = jnp.stack([2 * up, 2 * down + 1], axis=1)
    forward = [(order[i], order[(i + 1) % col_count]) for i in range(col_count)]
    backward = [(target, source) for source, target in forward]
    directions = (forward, backward)

    def gather_rows(own):
        found = {0: own}
        bit = row_count // 2
        while bit:
            pairs = [(i, i ^ bit) for i in range(row_count)]
            for key in list(found):
                found[key ^ bit] = [lax.ppermute(h, "row", pairs) for h in found[key]]
            bit //= 2
        return [h for key in range(row_count) for h in found[key]]

    for step in range(1, total_steps):
        parts = gather_rows(now)
        sent, _ = lax.optimization_barrier((later[step - 1], now[1]))
        came_weights = exchange(sent)
        value = None
        came = None
        for hop in range(col_count):
            chunk = chunks[hop]
            if hop:
                chunk, _ = lax.optimization_barrier((chunk, value))
            if hop == 1:
                chunk, came_weights = lax.optimization_barrier((chunk, came_weights))
            if hop:
                came = [lax.ppermute(v, "col", d) for v, d in zip(value, directions)]
            value = partial_sums(chunk, code, parts, blocks, half)
            if hop:
                value = [v + c.astype(jnp.float32) for v, c in zip(value, came)]
            if hop < col_count - 1:
                value = [v.astype(jnp.bfloat16) for v in value]
        weights = place(index[step], came_weights).astype(jnp.float32)
        weighted = [value[0] * weights[:, : piece // 2], value[1] * weights[:, piece // 2 :]]
        now = [w.astype(jnp.bfloat16) for w in weighted]

    total = jnp.sum(weighted[0], axis=1) + jnp.sum(weighted[1], axis=1)
    for axis, count in (("row", row_count), ("col", col_count)):
        bit = 1
        while bit < count:
            radix = min(4, count // bit)
            others = [
                lax.ppermute(total, axis, [(i, i ^ (bit * key)) for i in range(count)])
                for key in range(1, radix)
            ]
            total = total + others[0]
            if radix == 4:
                total = total + (others[1] + others[2])
            bit *= radix
    scale = total / states
    posterior = jnp.concatenate([w / scale[:, None] for w in weighted], axis=1)
    return posterior.astype(jnp.bfloat16), jnp.log(scale)


def solution(mesh):
    in_specs = (P("row", "col", None, None), P("row", "col"), P("col", "row"), P())
    out_specs = (P(None, ("row", "col")), P())
    return jax.shard_map(
        on_device, mesh=mesh, in_specs=in_specs, out_specs=out_specs, check_vma=False
    )
```

```python
import functools

import jax
import jax.numpy as jnp
from jax import lax
from jax.experimental import pallas as pl
from jax.experimental.pallas import tpu as pltpu
from jax.sharding import PartitionSpec as P

CAP = 26
CAP_PAD = 32
FOLD = 4


def line_schedule(length):
    orders = []
    for place in range(length):
        waiting = {block: length - abs(block - place) for block in range(length)}
        del waiting[place]
        order = [place]
        for slot in range(length - 1, 0, -1):
            block = max(waiting, key=lambda b: (waiting[b] == slot, waiting[b], b))
            del waiting[block]
            order.insert(0, block)
        orders.append(order)
    return orders


def pick_kernel(spans, ids_ref, table_ref, *refs):
    out_refs, staged = refs[:-1], refs[-1]
    rows = ids_ref.shape[0]
    vocab = table_ref.shape[0]
    wanted = lax.broadcasted_iota(jnp.int32, (rows, vocab), 1) == ids_ref[...]
    onehot = jnp.where(wanted, 1.0, 0.0).astype(jnp.bfloat16)
    value = jnp.dot(onehot, table_ref[...], preferred_element_type=jnp.float32)
    lanes = value.shape[1] // FOLD
    for low, out_ref in zip(spans, out_refs):
        for fold in range(FOLD):
            staged[fold * CAP : (fold + 1) * CAP, :] = value[
                low : low + CAP, fold * lanes : (fold + 1) * lanes
            ]
        out_ref[0] = staged[...].astype(out_ref.dtype)


def pick(ids, table, pieces):
    vocab, panel = table.shape
    steps, padded = ids.shape
    width = panel // pieces
    lanes = width // FOLD
    return pl.pallas_call(
        functools.partial(pick_kernel, [t * padded for t in range(steps)]),
        grid=(pieces,),
        in_specs=[
            pl.BlockSpec((steps * padded, 1), lambda i: (0, 0)),
            pl.BlockSpec((vocab, width), lambda i: (0, i)),
        ],
        out_specs=[pl.BlockSpec((1, FOLD * CAP, lanes), lambda i: (i, 0, 0))] * steps,
        out_shape=[jax.ShapeDtypeStruct((pieces, FOLD * CAP, lanes), table.dtype)] * steps,
        scratch_shapes=[pltpu.VMEM((FOLD * CAP, lanes), jnp.float32)],
        cost_estimate=pl.CostEstimate(
            flops=2 * steps * padded * vocab * width * pieces,
            bytes_accessed=2 * pieces * width * (vocab + steps * CAP),
            transcendentals=0,
        ),
        compiler_params=pltpu.CompilerParams(vmem_limit_bytes=40 << 20),
        name="pick",
    )(ids.reshape(-1, 1), table)


def fold_kernel(rows_ref, *out_refs):
    *out_refs, staged = out_refs
    lanes = staged.shape[1]
    for share, out_ref in enumerate(out_refs):
        for fold in range(FOLD):
            low = (share * FOLD + fold) * lanes
            staged[fold * CAP : (fold + 1) * CAP, :] = rows_ref[
                :CAP, low : low + lanes
            ].astype(jnp.float32)
        out_ref[0] = staged[...].astype(out_ref.dtype)


def fold_rows(rows, pieces, shares):
    padded, panel = rows.shape
    lanes = panel // pieces // shares // FOLD
    return pl.pallas_call(
        fold_kernel,
        grid=(pieces,),
        in_specs=[pl.BlockSpec((padded, panel // pieces), lambda i: (0, i))],
        out_specs=[pl.BlockSpec((1, FOLD * CAP, lanes), lambda i: (i, 0, 0))] * shares,
        out_shape=[jax.ShapeDtypeStruct((pieces, FOLD * CAP, lanes), rows.dtype)] * shares,
        scratch_shapes=[pltpu.VMEM((FOLD * CAP, lanes), jnp.float32)],
        cost_estimate=pl.CostEstimate(
            flops=0, bytes_accessed=4 * padded * panel, transcendentals=0
        ),
        compiler_params=pltpu.CompilerParams(vmem_limit_bytes=40 << 20),
        name="fold_rows",
    )(rows)


def place_kernel(index_ref, table_ref, out_ref):
    seqs = index_ref.shape[0]
    height = table_ref.shape[0]
    index = index_ref[...] + pl.program_id(0) * CAP
    wanted = lax.broadcasted_iota(jnp.int32, (seqs, height), 1) == index
    onehot = jnp.where(wanted, 1.0, 0.0).astype(jnp.bfloat16)
    out_ref[...] = jnp.dot(
        onehot, table_ref[...], preferred_element_type=jnp.float32
    ).astype(out_ref.dtype)


def place(index, messages):
    pieces, rows, lanes = messages.shape
    seqs = index.shape[0]
    return pl.pallas_call(
        place_kernel,
        grid=(FOLD,),
        in_specs=[
            pl.BlockSpec((seqs, 1), lambda i: (0, 0)),
            pl.BlockSpec((pieces * rows, lanes), lambda i: (0, 0)),
        ],
        out_specs=pl.BlockSpec((seqs, lanes), lambda i: (0, i)),
        out_shape=jax.ShapeDtypeStruct((seqs, FOLD * lanes), messages.dtype),
        cost_estimate=pl.CostEstimate(
            flops=2 * FOLD * seqs * pieces * rows * lanes,
            bytes_accessed=2 * lanes * (pieces * rows + FOLD * seqs),
            transcendentals=0,
        ),
        compiler_params=pltpu.CompilerParams(vmem_limit_bytes=40 << 20),
        name="place",
    )(index.reshape(-1, 1), messages.reshape(pieces * rows, lanes))


def partial_kernel(parts, chunk_ref, code_ref, *refs):
    part_refs, (blocks_ref, out_ref, held, sems) = refs[:parts], refs[parts:]
    step = pl.program_id(0)
    half, slots, width, _ = blocks_ref.shape
    piece_blocks = held.shape[2] // width

    @pl.when(step == 0)
    def _load():
        copies = []
        for number, part_ref in enumerate(part_refs):
            columns = part_ref.shape[1]
            copies.append(
                pltpu.make_async_copy(
                    part_ref,
                    held.at[number // 2, :, pl.ds(number % 2 * columns, columns)],
                    sems.at[number],
                )
            )
        for copy in copies:
            copy.start()
        for copy in copies:
            copy.wait()

    for block in range(half):
        total = None
        for slot in range(slots):
            code = code_ref[(chunk_ref[step] * half + block) * slots + slot]
            start = pl.multiple_of(code % piece_blocks * width, width)
            source = held[code // piece_blocks, :, pl.ds(start, width)]
            term = jnp.dot(
                source, blocks_ref[block, slot], preferred_element_type=jnp.float32
            )
            total = term if total is None else total + term
        out_ref[:, block * width : (block + 1) * width] = total.astype(out_ref.dtype)


def partial_sums(chunk, code, parts, blocks, half):
    _, slots, width, _ = blocks.shape
    seqs, columns = parts[0].shape
    count = len(parts)
    return pl.pallas_call(
        functools.partial(partial_kernel, count),
        grid_spec=pltpu.PrefetchScalarGridSpec(
            num_scalar_prefetch=2,
            grid=(2,),
            in_specs=[pl.BlockSpec(memory_space=pl.ANY)] * count
            + [
                pl.BlockSpec(
                    (half, slots, width, width),
                    lambda i, chunk, code: (chunk[i], 0, 0, 0),
                )
            ],
            out_specs=pl.BlockSpec((seqs, columns), lambda i, chunk, code: (0, i)),
            scratch_shapes=[
                pltpu.VMEM((count // 2, seqs, 2 * columns), jnp.bfloat16),
                pltpu.SemaphoreType.DMA((count,)),
            ],
        ),
        out_shape=jax.ShapeDtypeStruct((seqs, 2 * columns), parts[0].dtype),
        cost_estimate=pl.CostEstimate(
            flops=4 * half * slots * seqs * width * width,
            bytes_accessed=4 * half * slots * width * width + 2 * count * seqs * columns,
            transcendentals=0,
        ),
        compiler_params=pltpu.CompilerParams(vmem_limit_bytes=40 << 20),
        name="partial_sums",
    )(chunk, code, *parts, blocks)


def on_device(blocks, source_ids, emission, tokens):
    row_count = lax.axis_size("row")
    col_count = lax.axis_size("col")
    row_index = lax.axis_index("row")
    col_index = lax.axis_index("col")
    local_rows, local_slots, width, _ = blocks.shape
    vocab_local, panel = emission.shape
    piece = panel // col_count
    piece_blocks = piece // width
    half = piece_blocks // 2
    total_steps, seq_count = tokens.shape
    states = panel * row_count

    owner = tokens // vocab_local
    inner = tokens % vocab_local
    same = owner[:, :, None] == owner[:, None, :]
    earlier = jnp.arange(seq_count)[:, None] > jnp.arange(seq_count)[None, :]
    rank = jnp.sum((same & earlier[None]).astype(jnp.int32), axis=2)
    mine = (owner == col_index)[:, None, :] & (
        rank[:, None, :] == jnp.arange(CAP_PAD)[None, :, None]
    )
    ids = jnp.sum(jnp.where(mine, inner[:, None, :], 0), axis=2)
    index = owner * (FOLD * CAP) + rank

    def exchange(values):
        return lax.all_to_all(values, "col", 0, 0, tiled=True)

    first = jnp.take(emission, ids[0, :CAP], axis=0, mode="clip")
    (sent,) = fold_rows(first, col_count, 1)
    later = pick(ids[1:], emission, col_count)
    index_first, later = lax.optimization_barrier((index[0], later))
    start = place(index_first, exchange(sent))
    now = [start[:, : piece // 2], start[:, piece // 2 :]]

    group = source_ids // piece_blocks
    code = ((group // col_count) ^ row_index) * piece_blocks + source_ids % piece_blocks
    code = code.reshape(-1).astype(jnp.int32)

    line = col_count // 2
    spot, side = col_index // 2, col_index % 2
    orders = line_schedule(line)
    turn = jnp.array(orders, jnp.int32)[spot]
    halves = jnp.arange(2, dtype=jnp.int32)[None, :]
    send_chunks = 2 * (2 * turn + 1 - side)[:, None] + halves
    keep_chunks = 2 * (2 * turn + side)[:, None] + halves
    partners = [(i, i ^ 1) for i in range(col_count)]

    def line_pairs(spots, way):
        return [(2 * s + k, 2 * (s + way) + k) for s in spots for k in range(2)]

    def choose(blocks_of, reduced):
        rounds = {s: orders[s].index(b) for s, b in blocks_of.items()}
        value = None
        for number in sorted(set(rounds.values()), reverse=True):
            if value is None:
                value = reduced[number]
            else:
                wanted = functools.reduce(
                    jnp.logical_or, [spot == s for s in rounds if rounds[s] == number]
                )
                value = jnp.where(wanted, reduced[number], value)
        return value

    def add(*terms):
        total = functools.reduce(jnp.add, [t.astype(jnp.float32) for t in terms])
        return total.astype(jnp.bfloat16)

    def line_reduce(reduced):
        came = []
        for slot in range(1, line):
            reach = line - slot
            up = {s: s + reach for s in range(slot)}
            down = {s: s - reach for s in range(reach, line)}
            if slot < reach - 1:
                value = add(choose({**up, **down}, reduced), *came[:1])
                pairs = line_pairs(up, 1) + line_pairs(down, -1)
                came = [lax.ppermute(value, "col", pairs)] * 2
            else:
                values = [
                    add(choose(blocks_of, reduced), *came[way : way + 1])
                    for way, blocks_of in enumerate((up, down))
                ]
                came = [
                    lax.ppermute(values[0], "col", line_pairs(up, 1)),
                    lax.ppermute(values[1], "col", line_pairs(down, -1)),
                ]
        return came

    def gather_rows(own):
        found = {0: own}
        bit = row_count // 2
        while bit:
            pairs = [(i, i ^ bit) for i in range(row_count)]
            for key in list(found):
                found[key ^ bit] = [lax.ppermute(h, "row", pairs) for h in found[key]]
            bit //= 2
        return [h for key in range(row_count) for h in found[key]]

    for step in range(1, total_steps):
        parts = gather_rows(now)
        sent, _ = lax.optimization_barrier((later[step - 1], now[1]))
        came_weights = exchange(sent)
        sends, keeps, reduced = [], [], []
        for number in range(line):
            for ahead in range(len(sends), min(number + 2, line)):
                chunk = send_chunks[ahead]
                chunk, _ = lax.optimization_barrier((chunk, (sends[-1:], keeps[-1:])))
                sends.append(partial_sums(chunk, code, parts, blocks, half))
            before = sends[-1:] + keeps[-1:]
            if number == 0:
                before.append(came_weights)
            chunk, before = lax.optimization_barrier((keep_chunks[number], before))
            if number == 0:
                came_weights = before[-1]
            keeps.append(partial_sums(chunk, code, parts, blocks, half))
        swapped = [lax.ppermute(v, "col", partners) for v in sends]
        reduced = [add(k, v) for k, v in zip(keeps[:-1], swapped)]
        own = [keeps[-1], swapped[-1], *line_reduce(reduced)]
        value = functools.reduce(jnp.add, [v.astype(jnp.float32) for v in own])
        value = [value[:, : piece // 2], value[:, piece // 2 :]]
        weights = place(index[step], came_weights).astype(jnp.float32)
        weighted = [value[0] * weights[:, : piece // 2], value[1] * weights[:, piece // 2 :]]
        now = [w.astype(jnp.bfloat16) for w in weighted]

    total = jnp.sum(weighted[0], axis=1) + jnp.sum(weighted[1], axis=1)
    for axis, count in (("row", row_count), ("col", col_count)):
        bit = 1
        while bit < count:
            radix = min(4, count // bit)
            others = [
                lax.ppermute(total, axis, [(i, i ^ (bit * key)) for i in range(count)])
                for key in range(1, radix)
            ]
            total = total + others[0]
            if radix == 4:
                total = total + (others[1] + others[2])
            bit *= radix
    scale = total / states
    posterior = jnp.concatenate([w / scale[:, None] for w in weighted], axis=1)
    return posterior.astype(jnp.bfloat16), jnp.log(scale)


def solution(mesh):
    in_specs = (P("row", "col", None, None), P("row", "col"), P("col", "row"), P())
    out_specs = (P(None, ("row", "col")), P())
    return jax.shard_map(
        on_device, mesh=mesh, in_specs=in_specs, out_specs=out_specs, check_vma=False
    )
```

```python
import functools

import jax
import jax.numpy as jnp
from jax import lax
from jax.experimental import pallas as pl
from jax.experimental.pallas import tpu as pltpu
from jax.sharding import PartitionSpec as P

CAP = 26
CAP_PAD = 32
FOLD = 4
SUBLANES = 8


def ring_order(count):
    return list(range(0, count, 2)) + list(range(count - 1 - count % 2, 0, -2))


def pick_kernel(spans, ids_ref, table_ref, *refs):
    out_refs, staged = refs[:-1], refs[-1]
    rows = ids_ref.shape[0]
    vocab = table_ref.shape[0]
    wanted = lax.broadcasted_iota(jnp.int32, (rows, vocab), 1) == ids_ref[...]
    onehot = jnp.where(wanted, 1.0, 0.0).astype(jnp.bfloat16)
    value = jnp.dot(onehot, table_ref[...], preferred_element_type=jnp.float32)
    lanes = value.shape[1] // FOLD
    for low, out_ref in zip(spans, out_refs):
        for fold in range(FOLD):
            staged[fold * CAP : (fold + 1) * CAP, :] = value[
                low : low + CAP, fold * lanes : (fold + 1) * lanes
            ]
        out_ref[0] = staged[...].astype(out_ref.dtype)


def pick(ids, table, pieces):
    vocab, panel = table.shape
    steps, padded = ids.shape
    width = panel // pieces
    lanes = width // FOLD
    return pl.pallas_call(
        functools.partial(pick_kernel, [t * padded for t in range(steps)]),
        grid=(pieces,),
        in_specs=[
            pl.BlockSpec((steps * padded, 1), lambda i: (0, 0)),
            pl.BlockSpec((vocab, width), lambda i: (0, i)),
        ],
        out_specs=[pl.BlockSpec((1, FOLD * CAP, lanes), lambda i: (i, 0, 0))] * steps,
        out_shape=[jax.ShapeDtypeStruct((pieces, FOLD * CAP, lanes), table.dtype)] * steps,
        scratch_shapes=[pltpu.VMEM((FOLD * CAP, lanes), jnp.float32)],
        cost_estimate=pl.CostEstimate(
            flops=2 * steps * padded * vocab * width * pieces,
            bytes_accessed=2 * pieces * width * (vocab + steps * CAP),
            transcendentals=0,
        ),
        compiler_params=pltpu.CompilerParams(vmem_limit_bytes=40 << 20),
        name="pick",
    )(ids.reshape(-1, 1), table)


def fold_kernel(rows_ref, *out_refs):
    *out_refs, staged = out_refs
    lanes = staged.shape[1]
    for share, out_ref in enumerate(out_refs):
        for fold in range(FOLD):
            low = (share * FOLD + fold) * lanes
            staged[fold * CAP : (fold + 1) * CAP, :] = rows_ref[
                :CAP, low : low + lanes
            ].astype(jnp.float32)
        out_ref[0] = staged[...].astype(out_ref.dtype)


def fold_rows(rows, pieces, shares):
    padded, panel = rows.shape
    lanes = panel // pieces // shares // FOLD
    return pl.pallas_call(
        fold_kernel,
        grid=(pieces,),
        in_specs=[pl.BlockSpec((padded, panel // pieces), lambda i: (0, i))],
        out_specs=[pl.BlockSpec((1, FOLD * CAP, lanes), lambda i: (i, 0, 0))] * shares,
        out_shape=[jax.ShapeDtypeStruct((pieces, FOLD * CAP, lanes), rows.dtype)] * shares,
        scratch_shapes=[pltpu.VMEM((FOLD * CAP, lanes), jnp.float32)],
        cost_estimate=pl.CostEstimate(
            flops=0, bytes_accessed=4 * padded * panel, transcendentals=0
        ),
        compiler_params=pltpu.CompilerParams(vmem_limit_bytes=40 << 20),
        name="fold_rows",
    )(rows)


def place_kernel(index_ref, table_ref, out_ref):
    seqs = index_ref.shape[0]
    height = table_ref.shape[0]
    index = index_ref[...] + pl.program_id(0) * CAP
    wanted = lax.broadcasted_iota(jnp.int32, (seqs, height), 1) == index
    onehot = jnp.where(wanted, 1.0, 0.0).astype(jnp.bfloat16)
    out_ref[...] = jnp.dot(
        onehot, table_ref[...], preferred_element_type=jnp.float32
    ).astype(out_ref.dtype)


def place(index, messages):
    pieces, rows, lanes = messages.shape
    seqs = index.shape[0]
    return pl.pallas_call(
        place_kernel,
        grid=(FOLD,),
        in_specs=[
            pl.BlockSpec((seqs, 1), lambda i: (0, 0)),
            pl.BlockSpec((pieces * rows, lanes), lambda i: (0, 0)),
        ],
        out_specs=pl.BlockSpec((seqs, lanes), lambda i: (0, i)),
        out_shape=jax.ShapeDtypeStruct((seqs, FOLD * lanes), messages.dtype),
        cost_estimate=pl.CostEstimate(
            flops=2 * FOLD * seqs * pieces * rows * lanes,
            bytes_accessed=2 * lanes * (pieces * rows + FOLD * seqs),
            transcendentals=0,
        ),
        compiler_params=pltpu.CompilerParams(vmem_limit_bytes=40 << 20),
        name="place",
    )(index.reshape(-1, 1), messages.reshape(pieces * rows, lanes))


def partial_kernel(parts, chunk_ref, code_ref, *refs):
    part_refs, (blocks_ref, *out_refs, held, sems) = refs[:parts], refs[parts:]
    way, turn = pl.program_id(0), pl.program_id(1)
    count, slots, width, _ = blocks_ref.shape
    piece_blocks = held.shape[2] // width

    @pl.when((way == 0) & (turn == 0))
    def _load():
        copies = []
        for number, part_ref in enumerate(part_refs):
            columns = part_ref.shape[1]
            copies.append(
                pltpu.make_async_copy(
                    part_ref,
                    held.at[number // 2, :, pl.ds(number % 2 * columns, columns)],
                    sems.at[number],
                )
            )
        for copy in copies:
            copy.start()
        for copy in copies:
            copy.wait()

    totals = []
    for block in range(count):
        total = None
        for slot in range(slots):
            row = (chunk_ref[way] * pl.num_programs(1) + turn) * count + block
            code = code_ref[row * slots + slot]
            start = pl.multiple_of(code % piece_blocks * width, width)
            source = held[code // piece_blocks, :, pl.ds(start, width)]
            term = jnp.dot(
                source, blocks_ref[block, slot], preferred_element_type=jnp.float32
            )
            total = term if total is None else total + term
        totals.append(total.astype(jnp.bfloat16))

    for number, out_ref in enumerate(out_refs):

        @pl.when(way == number)
        def _store(out_ref=out_ref):
            for block, total in enumerate(totals):
                start = pl.multiple_of((turn * count + block) * width, width)
                out_ref[:, pl.ds(start, width)] = total


def partial_sums(chunk, code, parts, blocks, half):
    _, slots, width, _ = blocks.shape
    seqs, columns = parts[0].shape
    count = len(parts)
    turns = 2 if half % 2 == 0 else 1
    return pl.pallas_call(
        functools.partial(partial_kernel, count),
        grid_spec=pltpu.PrefetchScalarGridSpec(
            num_scalar_prefetch=2,
            grid=(2, turns),
            in_specs=[pl.BlockSpec(memory_space=pl.ANY)] * count
            + [
                pl.BlockSpec(
                    (half // turns, slots, width, width),
                    lambda i, j, chunk, code: (chunk[i] * turns + j, 0, 0, 0),
                )
            ],
            out_specs=[pl.BlockSpec((seqs, columns), lambda i, j, chunk, code: (0, 0))] * 2,
            scratch_shapes=[
                pltpu.VMEM((count // 2, seqs, 2 * columns), jnp.bfloat16),
                pltpu.SemaphoreType.DMA((count,)),
            ],
        ),
        out_shape=[jax.ShapeDtypeStruct((seqs, columns), jnp.bfloat16)] * 2,
        cost_estimate=pl.CostEstimate(
            flops=4 * half * slots * seqs * width * width,
            bytes_accessed=4 * half * slots * width * width + 2 * count * seqs * columns,
            transcendentals=0,
        ),
        compiler_params=pltpu.CompilerParams(vmem_limit_bytes=40 << 20),
        name="partial_sums",
    )(chunk, code, *parts, blocks)


def on_device(blocks, source_ids, emission, tokens):
    row_count = lax.axis_size("row")
    col_count = lax.axis_size("col")
    row_index = lax.axis_index("row")
    col_index = lax.axis_index("col")
    local_rows, local_slots, width, _ = blocks.shape
    vocab_local, panel = emission.shape
    piece = panel // col_count
    piece_blocks = piece // width
    half = piece_blocks // 2
    total_steps, seq_count = tokens.shape
    states = panel * row_count

    owner = tokens // vocab_local
    inner = tokens % vocab_local
    same = owner[:, :, None] == owner[:, None, :]
    earlier = jnp.arange(seq_count)[:, None] > jnp.arange(seq_count)[None, :]
    rank = jnp.sum((same & earlier[None]).astype(jnp.int32), axis=2)
    mine = (owner == col_index)[:, None, :] & (
        rank[:, None, :] == jnp.arange(CAP_PAD)[None, :, None]
    )
    ids = jnp.sum(jnp.where(mine, inner[:, None, :], 0), axis=2)
    index = owner * (FOLD * CAP) + rank

    def exchange(values):
        return lax.all_to_all(values, "col", 0, 0, tiled=True)

    first = jnp.take(emission, ids[0, :CAP], axis=0, mode="clip")
    (sent,) = fold_rows(first, col_count, 1)
    later = pick(ids[1:], emission, col_count)
    index_first, later = lax.optimization_barrier((index[0], later))
    start = place(index_first, exchange(sent))
    now = [start[:, : piece // 2], start[:, piece // 2 :]]

    group = source_ids // piece_blocks
    code = ((group // col_count) ^ row_index) * piece_blocks + source_ids % piece_blocks
    code = code.reshape(-1).astype(jnp.int32)

    order = ring_order(col_count)
    position = jnp.array([order.index(c) for c in range(col_count)], jnp.int32)[col_index]
    order_table = jnp.array(order, jnp.int32)
    hops = jnp.arange(col_count, dtype=jnp.int32)
    up = order_table[(position - 1 - hops) % col_count]
    down = order_table[(position + 1 + hops) % col_count]
    chunks = jnp.stack([2 * up, 2 * down + 1], axis=1)
    forward = [(order[i], order[(i + 1) % col_count]) for i in range(col_count)]
    backward = [(target, source) for source, target in forward]
    directions = (forward, backward)

    def gather_rows(own):
        found = {0: own}
        bit = row_count // 2
        while bit:
            pairs = [(i, i ^ bit) for i in range(row_count)]
            for key in list(found):
                found[key ^ bit] = [lax.ppermute(h, "row", pairs) for h in found[key]]
            bit //= 2
        return [h for key in range(row_count) for h in found[key]]

    for step in range(1, total_steps):
        parts = gather_rows(now)
        sent, _ = lax.optimization_barrier((later[step - 1], parts[2:4]))
        came_weights = exchange(sent)
        value = None
        for hop in range(col_count):
            chunk = chunks[hop]
            if hop:
                chunk, _ = lax.optimization_barrier((chunk, value))
            if hop == 1:
                chunk, came_weights = lax.optimization_barrier((chunk, came_weights))
            if hop:
                came = [lax.ppermute(v, "col", d) for v, d in zip(value, directions)]
            value = partial_sums(chunk, code, parts, blocks, half)
            if hop:
                value = [v.astype(jnp.float32) + c.astype(jnp.float32) for v, c in zip(value, came)]
            if hop < col_count - 1:
                value = [v.astype(jnp.bfloat16) for v in value]
        weights = place(index[step], came_weights).astype(jnp.float32)
        weighted = [value[0] * weights[:, : piece // 2], value[1] * weights[:, piece // 2 :]]
        now = [w.astype(jnp.bfloat16) for w in weighted]

    total = jnp.sum(weighted[0], axis=1) + jnp.sum(weighted[1], axis=1)
    devices = row_count * col_count
    totals = jnp.broadcast_to(total, (devices, SUBLANES, seq_count))
    totals = lax.all_to_all(totals, ("row", "col"), 0, 0, tiled=True)
    total = jnp.sum(totals[:, 0, :], axis=0)
    scale = total / states
    posterior = jnp.concatenate([w / scale[:, None] for w in weighted], axis=1)
    return posterior.astype(jnp.bfloat16), jnp.log(scale)


def solution(mesh):
    in_specs = (P("row", "col", None, None), P("row", "col"), P("col", "row"), P())
    out_specs = (P(None, ("row", "col")), P())
    return jax.shard_map(
        on_device, mesh=mesh, in_specs=in_specs, out_specs=out_specs, check_vma=False
    )
```

```python
import functools

import jax
import jax.numpy as jnp
from jax import lax
from jax.experimental import pallas as pl
from jax.experimental.pallas import tpu as pltpu
from jax.sharding import PartitionSpec as P

CAP = 26
CAP_PAD = 32
FOLD = 4
SUBLANES = 8


def ring_order(count):
    return list(range(0, count, 2)) + list(range(count - 1 - count % 2, 0, -2))


def pick_kernel(spans, ids_ref, table_ref, *refs):
    out_refs, staged = refs[:-1], refs[-1]
    rows = ids_ref.shape[0]
    vocab = table_ref.shape[0]
    wanted = lax.broadcasted_iota(jnp.int32, (rows, vocab), 1) == ids_ref[...]
    onehot = jnp.where(wanted, 1.0, 0.0).astype(jnp.bfloat16)
    value = jnp.dot(onehot, table_ref[...], preferred_element_type=jnp.float32)
    lanes = value.shape[1] // FOLD
    for low, out_ref in zip(spans, out_refs):
        for fold in range(FOLD):
            staged[fold * CAP : (fold + 1) * CAP, :] = value[
                low : low + CAP, fold * lanes : (fold + 1) * lanes
            ]
        out_ref[0] = staged[...].astype(out_ref.dtype)


def pick(ids, table, pieces):
    vocab, panel = table.shape
    steps, padded = ids.shape
    width = panel // pieces
    lanes = width // FOLD
    return pl.pallas_call(
        functools.partial(pick_kernel, [t * padded for t in range(steps)]),
        grid=(pieces,),
        in_specs=[
            pl.BlockSpec((steps * padded, 1), lambda i: (0, 0)),
            pl.BlockSpec((vocab, width), lambda i: (0, i)),
        ],
        out_specs=[pl.BlockSpec((1, FOLD * CAP, lanes), lambda i: (i, 0, 0))] * steps,
        out_shape=[jax.ShapeDtypeStruct((pieces, FOLD * CAP, lanes), table.dtype)] * steps,
        scratch_shapes=[pltpu.VMEM((FOLD * CAP, lanes), jnp.float32)],
        cost_estimate=pl.CostEstimate(
            flops=2 * steps * padded * vocab * width * pieces,
            bytes_accessed=2 * pieces * width * (vocab + steps * CAP),
            transcendentals=0,
        ),
        compiler_params=pltpu.CompilerParams(vmem_limit_bytes=40 << 20),
        name="pick",
    )(ids.reshape(-1, 1), table)


def fold_kernel(rows_ref, *out_refs):
    *out_refs, staged = out_refs
    lanes = staged.shape[1]
    for share, out_ref in enumerate(out_refs):
        for fold in range(FOLD):
            low = (share * FOLD + fold) * lanes
            staged[fold * CAP : (fold + 1) * CAP, :] = rows_ref[
                :CAP, low : low + lanes
            ].astype(jnp.float32)
        out_ref[0] = staged[...].astype(out_ref.dtype)


def fold_rows(rows, pieces, shares):
    padded, panel = rows.shape
    lanes = panel // pieces // shares // FOLD
    return pl.pallas_call(
        fold_kernel,
        grid=(pieces,),
        in_specs=[pl.BlockSpec((padded, panel // pieces), lambda i: (0, i))],
        out_specs=[pl.BlockSpec((1, FOLD * CAP, lanes), lambda i: (i, 0, 0))] * shares,
        out_shape=[jax.ShapeDtypeStruct((pieces, FOLD * CAP, lanes), rows.dtype)] * shares,
        scratch_shapes=[pltpu.VMEM((FOLD * CAP, lanes), jnp.float32)],
        cost_estimate=pl.CostEstimate(
            flops=0, bytes_accessed=4 * padded * panel, transcendentals=0
        ),
        compiler_params=pltpu.CompilerParams(vmem_limit_bytes=40 << 20),
        name="fold_rows",
    )(rows)


def place_kernel(index_ref, table_ref, out_ref):
    seqs = index_ref.shape[0]
    height = table_ref.shape[0]
    index = index_ref[...] + pl.program_id(0) * CAP
    wanted = lax.broadcasted_iota(jnp.int32, (seqs, height), 1) == index
    onehot = jnp.where(wanted, 1.0, 0.0).astype(jnp.bfloat16)
    out_ref[...] = jnp.dot(
        onehot, table_ref[...], preferred_element_type=jnp.float32
    ).astype(out_ref.dtype)


def place(index, messages):
    pieces, rows, lanes = messages.shape
    seqs = index.shape[0]
    return pl.pallas_call(
        place_kernel,
        grid=(FOLD,),
        in_specs=[
            pl.BlockSpec((seqs, 1), lambda i: (0, 0)),
            pl.BlockSpec((pieces * rows, lanes), lambda i: (0, 0)),
        ],
        out_specs=pl.BlockSpec((seqs, lanes), lambda i: (0, i)),
        out_shape=jax.ShapeDtypeStruct((seqs, FOLD * lanes), messages.dtype),
        cost_estimate=pl.CostEstimate(
            flops=2 * FOLD * seqs * pieces * rows * lanes,
            bytes_accessed=2 * lanes * (pieces * rows + FOLD * seqs),
            transcendentals=0,
        ),
        compiler_params=pltpu.CompilerParams(vmem_limit_bytes=40 << 20),
        name="place",
    )(index.reshape(-1, 1), messages.reshape(pieces * rows, lanes))


def lay_out(part_refs, held_ref, sems):
    quarter = held_ref.shape[2] // 4
    copies = []
    for number, part_ref in enumerate(part_refs):
        row, sub = number // 2, number % 2
        for way in range(2):
            copies.append(
                pltpu.make_async_copy(
                    part_ref.at[:, pl.ds(way * quarter, quarter)],
                    held_ref.at[row, :, pl.ds((2 * way + sub) * quarter, quarter)],
                    sems.at[2 * number + way],
                )
            )
    return copies


def partial_kernel(parts, chunk_ref, code_ref, *refs):
    if parts:
        part_refs, blocks_ref = refs[:parts], refs[parts]
        *out_refs, held_ref, buffer, sems, part_sems = refs[parts + 1 :]
        laid = lay_out(part_refs, held_ref, part_sems)
    else:
        held_ref, blocks_ref, *out_refs, buffer, sems = refs
        laid = []
    count, slots, width, _ = buffer.shape
    half = count // 2
    quarter = out_refs[0].shape[1]
    piece_blocks = held_ref.shape[2] // width
    rows = [chunk_ref[number // half] * half + number % half for number in range(count)]
    copies = [
        pltpu.make_async_copy(blocks_ref.at[row], buffer.at[number], sems.at[number])
        for number, row in enumerate(rows)
    ]
    for copy in laid + copies:
        copy.start()
    for copy in laid:
        copy.wait()
    for number, row in enumerate(rows):
        copies[number].wait()
        total = None
        for slot in range(slots):
            code = code_ref[row * slots + slot]
            start = pl.multiple_of(code % piece_blocks * width, width)
            source = held_ref[code // piece_blocks, :, pl.ds(start, width)]
            term = jnp.dot(
                source, buffer[number, slot], preferred_element_type=jnp.float32
            )
            total = term if total is None else total + term
        total = total.astype(jnp.bfloat16)
        way, low = number // half, number % half * width
        for sub in range(2):
            first = max(low, sub * quarter)
            last = min(low + width, (sub + 1) * quarter)
            if first < last:
                out_refs[2 * way + sub][:, first - sub * quarter : last - sub * quarter] = (
                    total[:, first - low : last - low]
                )


def partial_sums(chunk, code, sources, blocks, half):
    _, slots, width, _ = blocks.shape
    parts = len(sources) if isinstance(sources, list) else 0
    operands = sources if parts else [sources]
    rows = parts // 2 if parts else sources.shape[0]
    seqs, columns = sources[0].shape if parts else (sources.shape[1], sources.shape[2] // 2)
    quarter = jax.ShapeDtypeStruct((seqs, columns // 2), jnp.bfloat16)
    whole = jax.ShapeDtypeStruct((rows, seqs, 2 * columns), jnp.bfloat16)
    scratch = [
        pltpu.VMEM((2 * half, slots, width, width), blocks.dtype),
        pltpu.SemaphoreType.DMA((2 * half,)),
    ]
    if parts:
        scratch.append(pltpu.SemaphoreType.DMA((2 * parts,)))
    outs = [quarter] * 4 + ([whole] if parts else [])
    vmem = pl.BlockSpec(memory_space=pltpu.VMEM)
    smem = pl.BlockSpec(memory_space=pltpu.SMEM)
    anywhere = pl.BlockSpec(memory_space=pl.ANY)
    return pl.pallas_call(
        functools.partial(partial_kernel, parts),
        in_specs=[smem, smem] + ([anywhere] * parts if parts else [vmem]) + [anywhere],
        out_specs=[vmem] * len(outs),
        scratch_shapes=scratch,
        out_shape=outs,
        cost_estimate=pl.CostEstimate(
            flops=4 * half * slots * seqs * width * width,
            bytes_accessed=4 * half * slots * width * width + 8 * seqs * columns,
            transcendentals=0,
        ),
        compiler_params=pltpu.CompilerParams(vmem_limit_bytes=24 << 20),
        name="partial_sums",
    )(chunk, code, *operands, blocks)


def on_device(blocks, source_ids, emission, tokens):
    row_count = lax.axis_size("row")
    col_count = lax.axis_size("col")
    row_index = lax.axis_index("row")
    col_index = lax.axis_index("col")
    local_rows, local_slots, width, _ = blocks.shape
    vocab_local, panel = emission.shape
    piece = panel // col_count
    piece_blocks = piece // width
    half = piece_blocks // 2
    total_steps, seq_count = tokens.shape
    states = panel * row_count

    owner = tokens // vocab_local
    inner = tokens % vocab_local
    same = owner[:, :, None] == owner[:, None, :]
    earlier = jnp.arange(seq_count)[:, None] > jnp.arange(seq_count)[None, :]
    rank = jnp.sum((same & earlier[None]).astype(jnp.int32), axis=2)
    mine = (owner == col_index)[:, None, :] & (
        rank[:, None, :] == jnp.arange(CAP_PAD)[None, :, None]
    )
    ids = jnp.sum(jnp.where(mine, inner[:, None, :], 0), axis=2)
    index = owner * (FOLD * CAP) + rank

    def exchange(values):
        return lax.all_to_all(values, "col", 0, 0, tiled=True)

    first = jnp.take(emission, ids[0, :CAP], axis=0, mode="clip")
    (sent,) = fold_rows(first, col_count, 1)
    later = pick(ids[1:], emission, col_count)
    index_first, later = lax.optimization_barrier((index[0], later))
    start = place(index_first, exchange(sent))
    quarter = piece // 4

    def split(whole):
        return [whole[:, n * quarter : (n + 1) * quarter] for n in range(4)]

    def pair_up(values):
        return [jnp.concatenate([values[n], values[n + 2]], axis=1) for n in range(2)]

    now = pair_up(split(start))

    group = source_ids // piece_blocks
    code = ((group // col_count) ^ row_index) * piece_blocks + source_ids % piece_blocks
    code = code.reshape(-1).astype(jnp.int32)

    order = ring_order(col_count)
    position = jnp.array([order.index(c) for c in range(col_count)], jnp.int32)[col_index]
    order_table = jnp.array(order, jnp.int32)
    hops = jnp.arange(col_count, dtype=jnp.int32)
    up = order_table[(position - 1 - hops) % col_count]
    down = order_table[(position + 1 + hops) % col_count]
    chunks = jnp.stack([2 * up, 2 * down + 1], axis=1)
    forward = [(order[i], order[(i + 1) % col_count]) for i in range(col_count)]
    backward = [(target, source) for source, target in forward]
    directions = (forward, backward)

    def gather_rows(own):
        found = {0: own}
        bit = row_count // 2
        while bit:
            pairs = [(i, i ^ bit) for i in range(row_count)]
            for key in list(found):
                found[key ^ bit] = [lax.ppermute(h, "row", pairs) for h in found[key]]
            bit //= 2
        return [h for key in range(row_count) for h in found[key]]

    def add(mine, came):
        return (mine.astype(jnp.float32) + came.astype(jnp.float32)).astype(jnp.bfloat16)

    for step in range(1, total_steps):
        held = gather_rows(now)
        sent, _ = lax.optimization_barrier((later[step - 1], now[1]))
        came_weights = exchange(sent)
        value = None
        for hop in range(col_count):
            chunk = chunks[hop]
            if hop:
                chunk, _ = lax.optimization_barrier((chunk, value[0::2]))
            if hop == 2:
                chunk, came_weights = lax.optimization_barrier((chunk, came_weights))
            if hop:
                came = [lax.ppermute(v, "col", directions[n // 2]) for n, v in enumerate(value)]
            value = partial_sums(chunk, code, held, blocks, half)
            if not hop:
                *value, held = value
            if 0 < hop < col_count - 1:
                value = [add(v, c) if n % 2 == 0 else v for n, (v, c) in enumerate(zip(value, came))]
                came[1::2], _ = lax.optimization_barrier((came[1::2], value[0::2]))
                value = [add(v, c) if n % 2 else v for n, (v, c) in enumerate(zip(value, came))]
            elif hop:
                came[1::2], came[0::2] = lax.optimization_barrier((came[1::2], came[0::2]))
                value = [v.astype(jnp.float32) + c.astype(jnp.float32) for v, c in zip(value, came)]
        weights = split(place(index[step], came_weights))
        weighted = [v * w.astype(jnp.float32) for v, w in zip(value, weights)]
        now = pair_up([w.astype(jnp.bfloat16) for w in weighted])

    total = functools.reduce(jnp.add, [jnp.sum(w, axis=1) for w in weighted])
    devices = row_count * col_count
    totals = jnp.broadcast_to(total, (devices, SUBLANES, seq_count))
    totals = lax.all_to_all(totals, ("row", "col"), 0, 0, tiled=True)
    total = jnp.sum(totals[:, 0, :], axis=0)
    scale = total / states
    posterior = jnp.concatenate([w / scale[:, None] for w in weighted], axis=1)
    return posterior.astype(jnp.bfloat16), jnp.log(scale)


def solution(mesh):
    in_specs = (P("row", "col", None, None), P("row", "col"), P("col", "row"), P())
    out_specs = (P(None, ("row", "col")), P())
    return jax.shard_map(
        on_device, mesh=mesh, in_specs=in_specs, out_specs=out_specs, check_vma=False
    )
```

```python
import functools

import jax
import jax.numpy as jnp
from jax import lax
from jax.experimental import pallas as pl
from jax.experimental.pallas import tpu as pltpu
from jax.sharding import PartitionSpec as P

CAP = 26
CAP_PAD = 32
FOLD = 4
SUBLANES = 8


def ring_order(count):
    return list(range(0, count, 2)) + list(range(count - 1 - count % 2, 0, -2))


def pick_kernel(spans, ids_ref, table_ref, *refs):
    out_refs, staged = refs[:-1], refs[-1]
    rows = ids_ref.shape[0]
    vocab = table_ref.shape[0]
    wanted = lax.broadcasted_iota(jnp.int32, (rows, vocab), 1) == ids_ref[...]
    onehot = jnp.where(wanted, 1.0, 0.0).astype(jnp.bfloat16)
    value = jnp.dot(onehot, table_ref[...], preferred_element_type=jnp.float32)
    lanes = value.shape[1] // FOLD
    for low, out_ref in zip(spans, out_refs):
        for fold in range(FOLD):
            staged[fold * CAP : (fold + 1) * CAP, :] = value[
                low : low + CAP, fold * lanes : (fold + 1) * lanes
            ]
        out_ref[0] = staged[...].astype(out_ref.dtype)


def pick(ids, table, pieces):
    vocab, panel = table.shape
    steps, padded = ids.shape
    width = panel // pieces
    lanes = width // FOLD
    return pl.pallas_call(
        functools.partial(pick_kernel, [t * padded for t in range(steps)]),
        grid=(pieces,),
        in_specs=[
            pl.BlockSpec((steps * padded, 1), lambda i: (0, 0)),
            pl.BlockSpec((vocab, width), lambda i: (0, i)),
        ],
        out_specs=[pl.BlockSpec((1, FOLD * CAP, lanes), lambda i: (i, 0, 0))] * steps,
        out_shape=[jax.ShapeDtypeStruct((pieces, FOLD * CAP, lanes), table.dtype)] * steps,
        scratch_shapes=[pltpu.VMEM((FOLD * CAP, lanes), jnp.float32)],
        cost_estimate=pl.CostEstimate(
            flops=2 * steps * padded * vocab * width * pieces,
            bytes_accessed=2 * pieces * width * (vocab + steps * CAP),
            transcendentals=0,
        ),
        compiler_params=pltpu.CompilerParams(vmem_limit_bytes=20 << 20),
        name="pick",
    )(ids.reshape(-1, 1), table)


def fold_kernel(rows_ref, *refs):
    *out_refs, staged = refs
    lanes = staged.shape[1]
    for pair, out_ref in enumerate(out_refs):
        for fold in range(FOLD):
            low = 2 * lanes * (pair + 2 * (fold // 2)) + lanes * (fold % 2)
            staged[fold * CAP : (fold + 1) * CAP, :] = rows_ref[:, low : low + lanes].astype(
                jnp.float32
            )
        out_ref[0] = staged[...].astype(out_ref.dtype)


def fold_rows(rows, pieces):
    height, panel = rows.shape
    lanes = panel // pieces // 2 // FOLD
    return pl.pallas_call(
        fold_kernel,
        grid=(pieces,),
        in_specs=[pl.BlockSpec((height, panel // pieces), lambda i: (0, i))],
        out_specs=[pl.BlockSpec((1, FOLD * CAP, lanes), lambda i: (i, 0, 0))] * 2,
        out_shape=[jax.ShapeDtypeStruct((pieces, FOLD * CAP, lanes), rows.dtype)] * 2,
        scratch_shapes=[pltpu.VMEM((FOLD * CAP, lanes), jnp.float32)],
        cost_estimate=pl.CostEstimate(
            flops=0, bytes_accessed=4 * height * panel, transcendentals=0
        ),
        compiler_params=pltpu.CompilerParams(vmem_limit_bytes=16 << 20),
        name="fold_rows",
    )(rows)


def place_kernel(index_ref, table_ref, out_ref):
    seqs = index_ref.shape[0]
    height = table_ref.shape[0]
    index = index_ref[...] + pl.program_id(0) * CAP
    wanted = lax.broadcasted_iota(jnp.int32, (seqs, height), 1) == index
    onehot = jnp.where(wanted, 1.0, 0.0).astype(jnp.bfloat16)
    out_ref[...] = jnp.dot(
        onehot, table_ref[...], preferred_element_type=jnp.float32
    ).astype(out_ref.dtype)


def place(index, messages):
    pieces, rows, lanes = messages.shape
    seqs = index.shape[0]
    return pl.pallas_call(
        place_kernel,
        grid=(FOLD,),
        in_specs=[
            pl.BlockSpec((seqs, 1), lambda i: (0, 0)),
            pl.BlockSpec((pieces * rows, lanes), lambda i: (0, 0)),
        ],
        out_specs=pl.BlockSpec((seqs, lanes), lambda i: (0, i)),
        out_shape=jax.ShapeDtypeStruct((seqs, FOLD * lanes), messages.dtype),
        cost_estimate=pl.CostEstimate(
            flops=2 * FOLD * seqs * pieces * rows * lanes,
            bytes_accessed=2 * lanes * (pieces * rows + FOLD * seqs),
            transcendentals=0,
        ),
        compiler_params=pltpu.CompilerParams(vmem_limit_bytes=20 << 20),
        name="place",
    )(index.reshape(-1, 1), messages.reshape(pieces * rows, lanes))


def lay_out(part_refs, held_ref, sems):
    quarter = held_ref.shape[2] // 4
    copies = []
    for number, part_ref in enumerate(part_refs):
        row, sub = number // 2, number % 2
        for way in range(2):
            copies.append(
                pltpu.make_async_copy(
                    part_ref.at[:, pl.ds(way * quarter, quarter)],
                    held_ref.at[row, :, pl.ds((2 * way + sub) * quarter, quarter)],
                    sems.at[2 * number + way],
                )
            )
    return copies


def partial_kernel(parts, chunk_ref, code_ref, *refs):
    if parts:
        part_refs, blocks_ref = refs[:parts], refs[parts]
        *out_refs, held_ref, buffer, sems, part_sems = refs[parts + 1 :]
        laid = lay_out(part_refs, held_ref, part_sems)
    else:
        held_ref, blocks_ref, *out_refs, buffer, sems = refs
        laid = []
    count, slots, width, _ = buffer.shape
    half = count // 2
    quarter = out_refs[0].shape[1]
    piece_blocks = held_ref.shape[2] // width
    rows = [chunk_ref[number // half] * half + number % half for number in range(count)]
    copies = [
        pltpu.make_async_copy(blocks_ref.at[row], buffer.at[number], sems.at[number])
        for number, row in enumerate(rows)
    ]
    for copy in laid + copies:
        copy.start()
    for copy in laid:
        copy.wait()
    for number, row in enumerate(rows):
        copies[number].wait()
        total = None
        for slot in range(slots):
            code = code_ref[row * slots + slot]
            start = pl.multiple_of(code % piece_blocks * width, width)
            source = held_ref[code // piece_blocks, :, pl.ds(start, width)]
            term = jnp.dot(
                source, buffer[number, slot], preferred_element_type=jnp.float32
            )
            total = term if total is None else total + term
        total = total.astype(jnp.bfloat16)
        way, low = number // half, number % half * width
        for sub in range(2):
            first = max(low, sub * quarter)
            last = min(low + width, (sub + 1) * quarter)
            if first < last:
                out_refs[2 * way + sub][:, first - sub * quarter : last - sub * quarter] = (
                    total[:, first - low : last - low]
                )


def partial_sums(chunk, code, sources, blocks, half):
    _, slots, width, _ = blocks.shape
    parts = len(sources) if isinstance(sources, list) else 0
    operands = sources if parts else [sources]
    rows = parts // 2 if parts else sources.shape[0]
    seqs, columns = sources[0].shape if parts else (sources.shape[1], sources.shape[2] // 2)
    quarter = jax.ShapeDtypeStruct((seqs, columns // 2), jnp.bfloat16)
    whole = jax.ShapeDtypeStruct((rows, seqs, 2 * columns), jnp.bfloat16)
    scratch = [
        pltpu.VMEM((2 * half, slots, width, width), blocks.dtype),
        pltpu.SemaphoreType.DMA((2 * half,)),
    ]
    if parts:
        scratch.append(pltpu.SemaphoreType.DMA((2 * parts,)))
    outs = [quarter] * 4 + ([whole] if parts else [])
    vmem = pl.BlockSpec(memory_space=pltpu.VMEM)
    smem = pl.BlockSpec(memory_space=pltpu.SMEM)
    anywhere = pl.BlockSpec(memory_space=pl.ANY)
    return pl.pallas_call(
        functools.partial(partial_kernel, parts),
        in_specs=[smem, smem] + ([anywhere] * parts if parts else [vmem]) + [anywhere],
        out_specs=[vmem] * len(outs),
        scratch_shapes=scratch,
        out_shape=outs,
        cost_estimate=pl.CostEstimate(
            flops=4 * half * slots * seqs * width * width,
            bytes_accessed=4 * half * slots * width * width + 8 * seqs * columns,
            transcendentals=0,
        ),
        compiler_params=pltpu.CompilerParams(vmem_limit_bytes=16 << 20),
        name="partial_sums",
    )(chunk, code, *operands, blocks)


def on_device(blocks, source_ids, emission, tokens):
    row_count = lax.axis_size("row")
    col_count = lax.axis_size("col")
    row_index = lax.axis_index("row")
    col_index = lax.axis_index("col")
    local_rows, local_slots, width, _ = blocks.shape
    vocab_local, panel = emission.shape
    piece = panel // col_count
    piece_blocks = piece // width
    half = piece_blocks // 2
    total_steps, seq_count = tokens.shape
    states = panel * row_count

    owner = tokens // vocab_local
    inner = tokens % vocab_local
    same = owner[:, :, None] == owner[:, None, :]
    earlier = jnp.arange(seq_count)[:, None] > jnp.arange(seq_count)[None, :]
    rank = jnp.sum((same & earlier[None]).astype(jnp.int32), axis=2)
    mine = (owner == col_index)[:, None, :] & (
        rank[:, None, :] == jnp.arange(CAP_PAD)[None, :, None]
    )
    ids = jnp.sum(jnp.where(mine, inner[:, None, :], 0), axis=2)
    index = owner * (FOLD * CAP) + rank

    def exchange(values):
        return lax.all_to_all(values, "col", 0, 0, tiled=True)

    first = jnp.take(emission, ids[0, :CAP], axis=0, mode="clip")
    sent_pairs = fold_rows(first, col_count)
    ids_later, sent_pairs = lax.optimization_barrier((ids[1:], sent_pairs))
    later = pick(ids_later, emission, col_count)
    quarter = piece // 4

    def split(whole):
        return [whole[:, n * quarter : (n + 1) * quarter] for n in range(4)]

    def gather_rows(own):
        found = {0: own}
        bit = row_count // 2
        while bit:
            pairs = [(i, i ^ bit) for i in range(row_count)]
            for key in list(found):
                found[key ^ bit] = lax.ppermute(found[key], "row", pairs)
            bit //= 2
        return [found[key] for key in range(row_count)]

    index_first, later = lax.optimization_barrier((index[0], later))
    start_a = place(index_first, exchange(sent_pairs[0]))
    held_a = gather_rows(start_a)
    came_b, _ = lax.optimization_barrier((exchange(sent_pairs[1]), held_a))
    start_b = place(index_first, came_b)
    held_pairs = [held_a, gather_rows(start_b)]
    ready = start_b

    group = source_ids // piece_blocks
    code = ((group // col_count) ^ row_index) * piece_blocks + source_ids % piece_blocks
    code = code.reshape(-1).astype(jnp.int32)

    order = ring_order(col_count)
    position = jnp.array([order.index(c) for c in range(col_count)], jnp.int32)[col_index]
    order_table = jnp.array(order, jnp.int32)
    hops = jnp.arange(col_count, dtype=jnp.int32)
    up = order_table[(position - 1 - hops) % col_count]
    down = order_table[(position + 1 + hops) % col_count]
    chunks = jnp.stack([2 * up, 2 * down + 1], axis=1)
    forward = [(order[i], order[(i + 1) % col_count]) for i in range(col_count)]
    backward = [(target, source) for source, target in forward]
    directions = (forward, backward)

    def add(mine, came):
        return (mine.astype(jnp.float32) + came.astype(jnp.float32)).astype(jnp.bfloat16)

    for step in range(1, total_steps):
        sent, _ = lax.optimization_barrier((later[step - 1], ready))
        came_weights = exchange(sent)
        held = [pair[key] for key in range(row_count) for pair in held_pairs]
        *value, held = partial_sums(chunks[0], code, held, blocks, half)
        for hop in range(1, col_count):
            came = [lax.ppermute(v, "col", directions[n // 2]) for n, v in enumerate(value)]
            if hop == col_count - 1:
                break
            chunk, _ = lax.optimization_barrier((chunks[hop], value[0::2]))
            if hop == 2:
                chunk, came_weights, own = lax.optimization_barrier((chunk, came_weights, own))
            value = list(partial_sums(chunk, code, held, blocks, half))
            if hop == 1:
                chunk, _ = lax.optimization_barrier((chunks[-1], value))
                own = partial_sums(chunk, code, held, blocks, half)
            value[0::2] = [add(v, c) for v, c in zip(value[0::2], came[0::2])]
            came[1::2], _ = lax.optimization_barrier((came[1::2], value[0::2]))
            value[1::2] = [add(v, c) for v, c in zip(value[1::2], came[1::2])]
        weights = split(place(index[step], came_weights))
        weighted = [None] * 4
        held_pairs = []
        for pair in range(2):
            for n in (pair, pair + 2):
                carried = own[n].astype(jnp.float32) + came[n].astype(jnp.float32)
                weighted[n] = carried * weights[n].astype(jnp.float32)
            if step < total_steps - 1:
                now = jnp.concatenate(
                    [weighted[n].astype(jnp.bfloat16) for n in (pair, pair + 2)], axis=1
                )
                held_pairs.append(gather_rows(now))
                if pair == 0:
                    ready = now
                    came[1::2], _ = lax.optimization_barrier((came[1::2], now))

    total = functools.reduce(jnp.add, [jnp.sum(w, axis=1) for w in weighted])
    devices = row_count * col_count
    totals = jnp.broadcast_to(total, (devices, SUBLANES, seq_count))
    totals = lax.all_to_all(totals, ("row", "col"), 0, 0, tiled=True)
    total = jnp.sum(totals[:, 0, :], axis=0)
    scale = total / states
    posterior = jnp.concatenate([w / scale[:, None] for w in weighted], axis=1)
    return posterior.astype(jnp.bfloat16), jnp.log(scale)


def solution(mesh):
    in_specs = (P("row", "col", None, None), P("row", "col"), P("col", "row"), P())
    out_specs = (P(None, ("row", "col")), P())
    return jax.shard_map(
        on_device, mesh=mesh, in_specs=in_specs, out_specs=out_specs, check_vma=False
    )
```

```python
import functools

import jax
import jax.numpy as jnp
from jax import lax
from jax.experimental import pallas as pl
from jax.experimental.pallas import tpu as pltpu
from jax.sharding import PartitionSpec as P

CAP = 26
CAP_PAD = 32
FOLD = 4
SUBLANES = 8


def ring_order(count):
    return list(range(0, count, 2)) + list(range(count - 1 - count % 2, 0, -2))


def pick_kernel(spans, ids_ref, table_ref, *refs):
    out_refs, staged = refs[:-1], refs[-1]
    rows = ids_ref.shape[0]
    vocab = table_ref.shape[0]
    wanted = lax.broadcasted_iota(jnp.int32, (rows, vocab), 1) == ids_ref[...]
    onehot = jnp.where(wanted, 1.0, 0.0).astype(jnp.bfloat16)
    value = jnp.dot(onehot, table_ref[...], preferred_element_type=jnp.float32)
    lanes = value.shape[1] // FOLD
    for low, out_ref in zip(spans, out_refs):
        for fold in range(FOLD):
            staged[fold * CAP : (fold + 1) * CAP, :] = value[
                low : low + CAP, fold * lanes : (fold + 1) * lanes
            ]
        out_ref[0] = staged[...].astype(out_ref.dtype)


def pick(ids, table, pieces):
    vocab, panel = table.shape
    steps, padded = ids.shape
    width = panel // pieces
    lanes = width // FOLD
    return pl.pallas_call(
        functools.partial(pick_kernel, [t * padded for t in range(steps)]),
        grid=(pieces,),
        in_specs=[
            pl.BlockSpec((steps * padded, 1), lambda i: (0, 0)),
            pl.BlockSpec((vocab, width), lambda i: (0, i)),
        ],
        out_specs=[pl.BlockSpec((1, FOLD * CAP, lanes), lambda i: (i, 0, 0))] * steps,
        out_shape=[jax.ShapeDtypeStruct((pieces, FOLD * CAP, lanes), table.dtype)] * steps,
        scratch_shapes=[pltpu.VMEM((FOLD * CAP, lanes), jnp.float32)],
        cost_estimate=pl.CostEstimate(
            flops=2 * steps * padded * vocab * width * pieces,
            bytes_accessed=2 * pieces * width * (vocab + steps * CAP),
            transcendentals=0,
        ),
        compiler_params=pltpu.CompilerParams(vmem_limit_bytes=40 << 20),
        name="pick",
    )(ids.reshape(-1, 1), table)


def fold_kernel(rows_ref, *refs):
    *out_refs, staged = refs
    lanes = staged.shape[1]
    for pair, out_ref in enumerate(out_refs):
        for fold in range(FOLD):
            low = 2 * lanes * (pair + 2 * (fold // 2)) + lanes * (fold % 2)
            staged[fold * CAP : (fold + 1) * CAP, :] = rows_ref[:, low : low + lanes].astype(
                jnp.float32
            )
        out_ref[0] = staged[...].astype(out_ref.dtype)


def fold_rows(rows, pieces):
    height, panel = rows.shape
    lanes = panel // pieces // 2 // FOLD
    return pl.pallas_call(
        fold_kernel,
        grid=(pieces,),
        in_specs=[pl.BlockSpec((height, panel // pieces), lambda i: (0, i))],
        out_specs=[pl.BlockSpec((1, FOLD * CAP, lanes), lambda i: (i, 0, 0))] * 2,
        out_shape=[jax.ShapeDtypeStruct((pieces, FOLD * CAP, lanes), rows.dtype)] * 2,
        scratch_shapes=[pltpu.VMEM((FOLD * CAP, lanes), jnp.float32)],
        cost_estimate=pl.CostEstimate(
            flops=0, bytes_accessed=4 * height * panel, transcendentals=0
        ),
        compiler_params=pltpu.CompilerParams(vmem_limit_bytes=16 << 20),
        name="fold_rows",
    )(rows)


def place_kernel(index_ref, table_ref, out_ref):
    seqs = index_ref.shape[0]
    height = table_ref.shape[0]
    index = index_ref[...] + pl.program_id(0) * CAP
    wanted = lax.broadcasted_iota(jnp.int32, (seqs, height), 1) == index
    onehot = jnp.where(wanted, 1.0, 0.0).astype(jnp.bfloat16)
    out_ref[...] = jnp.dot(
        onehot, table_ref[...], preferred_element_type=jnp.float32
    ).astype(out_ref.dtype)


def place(index, messages):
    pieces, rows, lanes = messages.shape
    seqs = index.shape[0]
    return pl.pallas_call(
        place_kernel,
        grid=(FOLD,),
        in_specs=[
            pl.BlockSpec((seqs, 1), lambda i: (0, 0)),
            pl.BlockSpec((pieces * rows, lanes), lambda i: (0, 0)),
        ],
        out_specs=pl.BlockSpec((seqs, lanes), lambda i: (0, i)),
        out_shape=jax.ShapeDtypeStruct((seqs, FOLD * lanes), messages.dtype),
        cost_estimate=pl.CostEstimate(
            flops=2 * FOLD * seqs * pieces * rows * lanes,
            bytes_accessed=2 * lanes * (pieces * rows + FOLD * seqs),
            transcendentals=0,
        ),
        compiler_params=pltpu.CompilerParams(vmem_limit_bytes=40 << 20),
        name="place",
    )(index.reshape(-1, 1), messages.reshape(pieces * rows, lanes))


def lay_out(part_refs, held_ref, sems):
    quarter = held_ref.shape[2] // 4
    copies = []
    for number, part_ref in enumerate(part_refs):
        row, sub = number // 2, number % 2
        for way in range(2):
            copies.append(
                pltpu.make_async_copy(
                    part_ref.at[:, pl.ds(way * quarter, quarter)],
                    held_ref.at[row, :, pl.ds((2 * way + sub) * quarter, quarter)],
                    sems.at[2 * number + way],
                )
            )
    return copies


def partial_kernel(parts, chunk_ref, code_ref, *refs):
    if parts:
        part_refs, blocks_ref = refs[:parts], refs[parts]
        *out_refs, held_ref, buffer, sems, part_sems = refs[parts + 1 :]
        laid = lay_out(part_refs, held_ref, part_sems)
    else:
        held_ref, blocks_ref, *out_refs, buffer, sems = refs
        laid = []
    count, slots, width, _ = buffer.shape
    half = count // 2
    quarter = out_refs[0].shape[1]
    piece_blocks = held_ref.shape[2] // width
    rows = [chunk_ref[number // half] * half + number % half for number in range(count)]
    copies = [
        pltpu.make_async_copy(blocks_ref.at[row], buffer.at[number], sems.at[number])
        for number, row in enumerate(rows)
    ]
    for copy in laid + copies:
        copy.start()
    for copy in laid:
        copy.wait()
    for number, row in enumerate(rows):
        copies[number].wait()
        total = None
        for slot in range(slots):
            code = code_ref[row * slots + slot]
            start = pl.multiple_of(code % piece_blocks * width, width)
            source = held_ref[code // piece_blocks, :, pl.ds(start, width)]
            term = jnp.dot(
                source, buffer[number, slot], preferred_element_type=jnp.float32
            )
            total = term if total is None else total + term
        total = total.astype(jnp.bfloat16)
        way, low = number // half, number % half * width
        for sub in range(2):
            first = max(low, sub * quarter)
            last = min(low + width, (sub + 1) * quarter)
            if first < last:
                out_refs[2 * way + sub][:, first - sub * quarter : last - sub * quarter] = (
                    total[:, first - low : last - low]
                )


def partial_sums(chunk, code, sources, blocks, half):
    _, slots, width, _ = blocks.shape
    parts = len(sources) if isinstance(sources, list) else 0
    operands = sources if parts else [sources]
    rows = parts // 2 if parts else sources.shape[0]
    seqs, columns = sources[0].shape if parts else (sources.shape[1], sources.shape[2] // 2)
    quarter = jax.ShapeDtypeStruct((seqs, columns // 2), jnp.bfloat16)
    whole = jax.ShapeDtypeStruct((rows, seqs, 2 * columns), jnp.bfloat16)
    scratch = [
        pltpu.VMEM((2 * half, slots, width, width), blocks.dtype),
        pltpu.SemaphoreType.DMA((2 * half,)),
    ]
    if parts:
        scratch.append(pltpu.SemaphoreType.DMA((2 * parts,)))
    outs = [quarter] * 4 + ([whole] if parts else [])
    vmem = pl.BlockSpec(memory_space=pltpu.VMEM)
    smem = pl.BlockSpec(memory_space=pltpu.SMEM)
    anywhere = pl.BlockSpec(memory_space=pl.ANY)
    return pl.pallas_call(
        functools.partial(partial_kernel, parts),
        in_specs=[smem, smem] + ([anywhere] * parts if parts else [vmem]) + [anywhere],
        out_specs=[vmem] * len(outs),
        scratch_shapes=scratch,
        out_shape=outs,
        cost_estimate=pl.CostEstimate(
            flops=4 * half * slots * seqs * width * width,
            bytes_accessed=4 * half * slots * width * width + 8 * seqs * columns,
            transcendentals=0,
        ),
        compiler_params=pltpu.CompilerParams(vmem_limit_bytes=24 << 20),
        name="partial_sums",
    )(chunk, code, *operands, blocks)


def on_device(blocks, source_ids, emission, tokens):
    row_count = lax.axis_size("row")
    col_count = lax.axis_size("col")
    row_index = lax.axis_index("row")
    col_index = lax.axis_index("col")
    local_rows, local_slots, width, _ = blocks.shape
    vocab_local, panel = emission.shape
    piece = panel // col_count
    piece_blocks = piece // width
    half = piece_blocks // 2
    total_steps, seq_count = tokens.shape
    states = panel * row_count

    owner = tokens // vocab_local
    inner = tokens % vocab_local
    same = owner[:, :, None] == owner[:, None, :]
    earlier = jnp.arange(seq_count)[:, None] > jnp.arange(seq_count)[None, :]
    rank = jnp.sum((same & earlier[None]).astype(jnp.int32), axis=2)
    mine = (owner == col_index)[:, None, :] & (
        rank[:, None, :] == jnp.arange(CAP_PAD)[None, :, None]
    )
    ids = jnp.sum(jnp.where(mine, inner[:, None, :], 0), axis=2)
    index = owner * (FOLD * CAP) + rank

    def exchange(values):
        return lax.all_to_all(values, "col", 0, 0, tiled=True)

    first = jnp.take(emission, ids[0, :CAP], axis=0, mode="clip")
    sent_pairs = fold_rows(first, col_count)
    ids_later, sent_pairs = lax.optimization_barrier((ids[1:], sent_pairs))
    later = pick(ids_later, emission, col_count)
    quarter = piece // 4

    def split(whole):
        return [whole[:, n * quarter : (n + 1) * quarter] for n in range(4)]

    def gather_rows(own):
        found = {0: own}
        bit = row_count // 2
        while bit:
            pairs = [(i, i ^ bit) for i in range(row_count)]
            for key in list(found):
                found[key ^ bit] = lax.ppermute(found[key], "row", pairs)
            bit //= 2
        return [found[key] for key in range(row_count)]

    sent_b, later, index_first = lax.optimization_barrier((sent_pairs[1], later, index[0]))
    start_a = place(index_first, exchange(sent_pairs[0]))
    held_a = gather_rows(start_a)
    came_b, _ = lax.optimization_barrier((exchange(sent_b), held_a))
    start_b = place(index_first, came_b)
    held_pairs = [held_a, gather_rows(start_b)]
    ready = start_b

    group = source_ids // piece_blocks
    code = ((group // col_count) ^ row_index) * piece_blocks + source_ids % piece_blocks
    code = code.reshape(-1).astype(jnp.int32)

    order = ring_order(col_count)
    position = jnp.array([order.index(c) for c in range(col_count)], jnp.int32)[col_index]
    order_table = jnp.array(order, jnp.int32)
    hops = jnp.arange(col_count, dtype=jnp.int32)
    up = order_table[(position - 1 - hops) % col_count]
    down = order_table[(position + 1 + hops) % col_count]
    chunks = jnp.stack([2 * up, 2 * down + 1], axis=1)
    forward = [(order[i], order[(i + 1) % col_count]) for i in range(col_count)]
    backward = [(target, source) for source, target in forward]
    directions = (forward, backward)

    def add(mine, came):
        return (mine.astype(jnp.float32) + came.astype(jnp.float32)).astype(jnp.bfloat16)

    for step in range(1, total_steps):
        sent, _ = lax.optimization_barrier((later[step - 1], ready))
        came_weights = exchange(sent)
        held = [pair[key] for key in range(row_count) for pair in held_pairs]
        *value, held = partial_sums(chunks[0], code, held, blocks, half)
        for hop in range(1, col_count):
            came = [lax.ppermute(v, "col", directions[n // 2]) for n, v in enumerate(value)]
            if hop == col_count - 1:
                break
            chunk, _ = lax.optimization_barrier((chunks[hop], value[0::2]))
            if hop == 2:
                chunk, came_weights, own = lax.optimization_barrier((chunk, came_weights, own))
            value = list(partial_sums(chunk, code, held, blocks, half))
            if hop == 1:
                chunk, _ = lax.optimization_barrier((chunks[-1], value))
                own = partial_sums(chunk, code, held, blocks, half)
            value[0::2] = [add(v, c) for v, c in zip(value[0::2], came[0::2])]
            came[1::2], _ = lax.optimization_barrier((came[1::2], value[0::2]))
            value[1::2] = [add(v, c) for v, c in zip(value[1::2], came[1::2])]
        weights = split(place(index[step], came_weights))
        weighted = [None] * 4
        came[1::2], came[0::2] = lax.optimization_barrier((came[1::2], came[0::2]))
        for n in range(4):
            carried = own[n].astype(jnp.float32) + came[n].astype(jnp.float32)
            weighted[n] = carried * weights[n].astype(jnp.float32)
        if step < total_steps - 1:
            now = [w.astype(jnp.bfloat16) for w in weighted]
            now = [jnp.concatenate(now[pair::2], axis=1) for pair in range(2)]
            held_pairs = [gather_rows(pair) for pair in now]
            ready = now[1]

    total = functools.reduce(jnp.add, [jnp.sum(w, axis=1) for w in weighted])
    devices = row_count * col_count
    totals = jnp.broadcast_to(total, (devices, SUBLANES, seq_count))
    totals = lax.all_to_all(totals, ("row", "col"), 0, 0, tiled=True)
    total = jnp.sum(totals[:, 0, :], axis=0)
    scale = total / states
    posterior = jnp.concatenate([w / scale[:, None] for w in weighted], axis=1)
    return posterior.astype(jnp.bfloat16), jnp.log(scale)


def solution(mesh):
    in_specs = (P("row", "col", None, None), P("row", "col"), P("col", "row"), P())
    out_specs = (P(None, ("row", "col")), P())
    return jax.shard_map(
        on_device, mesh=mesh, in_specs=in_specs, out_specs=out_specs, check_vma=False
    )
```

```python
import functools

import jax
import jax.numpy as jnp
from jax import lax
from jax.experimental import pallas as pl
from jax.experimental.pallas import tpu as pltpu
from jax.sharding import PartitionSpec as P

CAP = 26
CAP_PAD = 32
FOLD = 4
SUBLANES = 8


def ring_order(count):
    return list(range(0, count, 2)) + list(range(count - 1 - count % 2, 0, -2))


def pick_kernel(spans, ids_ref, table_ref, *refs):
    out_refs, staged = refs[:-1], refs[-1]
    rows = ids_ref.shape[0]
    vocab = table_ref.shape[0]
    wanted = lax.broadcasted_iota(jnp.int32, (rows, vocab), 1) == ids_ref[...]
    onehot = jnp.where(wanted, 1.0, 0.0).astype(jnp.bfloat16)
    value = jnp.dot(onehot, table_ref[...], preferred_element_type=jnp.float32)
    lanes = value.shape[1] // FOLD
    for low, out_ref in zip(spans, out_refs):
        for fold in range(FOLD):
            staged[fold * CAP : (fold + 1) * CAP, :] = value[
                low : low + CAP, fold * lanes : (fold + 1) * lanes
            ]
        out_ref[0] = staged[...].astype(out_ref.dtype)


def pick(ids, table, pieces):
    vocab, panel = table.shape
    steps, padded = ids.shape
    width = panel // pieces
    lanes = width // FOLD
    return pl.pallas_call(
        functools.partial(pick_kernel, [t * padded for t in range(steps)]),
        grid=(pieces,),
        in_specs=[
            pl.BlockSpec((steps * padded, 1), lambda i: (0, 0)),
            pl.BlockSpec((vocab, width), lambda i: (0, i)),
        ],
        out_specs=[pl.BlockSpec((1, FOLD * CAP, lanes), lambda i: (i, 0, 0))] * steps,
        out_shape=[jax.ShapeDtypeStruct((pieces, FOLD * CAP, lanes), table.dtype)] * steps,
        scratch_shapes=[pltpu.VMEM((FOLD * CAP, lanes), jnp.float32)],
        cost_estimate=pl.CostEstimate(
            flops=2 * steps * padded * vocab * width * pieces,
            bytes_accessed=2 * pieces * width * (vocab + steps * CAP),
            transcendentals=0,
        ),
        compiler_params=pltpu.CompilerParams(vmem_limit_bytes=40 << 20),
        name="pick",
    )(ids.reshape(-1, 1), table)


def fold_kernel(rows_ref, *refs):
    *out_refs, staged = refs
    lanes = staged.shape[1]
    for pair, out_ref in enumerate(out_refs):
        for fold in range(FOLD):
            low = 2 * lanes * (pair + 2 * (fold // 2)) + lanes * (fold % 2)
            staged[fold * CAP : (fold + 1) * CAP, :] = rows_ref[:, low : low + lanes].astype(
                jnp.float32
            )
        out_ref[0] = staged[...].astype(out_ref.dtype)


def fold_rows(rows, pieces):
    height, panel = rows.shape
    lanes = panel // pieces // 2 // FOLD
    return pl.pallas_call(
        fold_kernel,
        grid=(pieces,),
        in_specs=[pl.BlockSpec((height, panel // pieces), lambda i: (0, i))],
        out_specs=[pl.BlockSpec((1, FOLD * CAP, lanes), lambda i: (i, 0, 0))] * 2,
        out_shape=[jax.ShapeDtypeStruct((pieces, FOLD * CAP, lanes), rows.dtype)] * 2,
        scratch_shapes=[pltpu.VMEM((FOLD * CAP, lanes), jnp.float32)],
        cost_estimate=pl.CostEstimate(
            flops=0, bytes_accessed=4 * height * panel, transcendentals=0
        ),
        compiler_params=pltpu.CompilerParams(vmem_limit_bytes=16 << 20),
        name="fold_rows",
    )(rows)


def place_kernel(index_ref, table_ref, out_ref):
    seqs = index_ref.shape[0]
    height = table_ref.shape[0]
    index = index_ref[...] + pl.program_id(0) * CAP
    wanted = lax.broadcasted_iota(jnp.int32, (seqs, height), 1) == index
    onehot = jnp.where(wanted, 1.0, 0.0).astype(jnp.bfloat16)
    out_ref[...] = jnp.dot(
        onehot, table_ref[...], preferred_element_type=jnp.float32
    ).astype(out_ref.dtype)


def place(index, messages):
    pieces, rows, lanes = messages.shape
    seqs = index.shape[0]
    return pl.pallas_call(
        place_kernel,
        grid=(FOLD,),
        in_specs=[
            pl.BlockSpec((seqs, 1), lambda i: (0, 0)),
            pl.BlockSpec((pieces * rows, lanes), lambda i: (0, 0)),
        ],
        out_specs=pl.BlockSpec((seqs, lanes), lambda i: (0, i)),
        out_shape=jax.ShapeDtypeStruct((seqs, FOLD * lanes), messages.dtype),
        cost_estimate=pl.CostEstimate(
            flops=2 * FOLD * seqs * pieces * rows * lanes,
            bytes_accessed=2 * lanes * (pieces * rows + FOLD * seqs),
            transcendentals=0,
        ),
        compiler_params=pltpu.CompilerParams(vmem_limit_bytes=40 << 20),
        name="place",
    )(index.reshape(-1, 1), messages.reshape(pieces * rows, lanes))


def lay_out(part_refs, held_ref, sems):
    quarter = held_ref.shape[2] // 4
    copies = []
    for number, part_ref in enumerate(part_refs):
        row, sub = number // 2, number % 2
        for way in range(2):
            copies.append(
                pltpu.make_async_copy(
                    part_ref.at[:, pl.ds(way * quarter, quarter)],
                    held_ref.at[row, :, pl.ds((2 * way + sub) * quarter, quarter)],
                    sems.at[2 * number + way],
                )
            )
    return copies


def partial_kernel(parts, chunk_ref, code_ref, *refs):
    if parts:
        part_refs, blocks_ref = refs[:parts], refs[parts]
        *out_refs, whole_ref, held_ref, buffer, sems, held_sems = refs[parts + 1 :]
        laid = lay_out(part_refs, held_ref, held_sems)
        kept = [pltpu.make_async_copy(held_ref, whole_ref, held_sems.at[2 * parts])]
    else:
        whole_ref, blocks_ref, *out_refs, held_ref, buffer, sems, held_sems = refs
        laid = [pltpu.make_async_copy(whole_ref, held_ref, held_sems.at[0])]
        kept = []
    count, slots, width, _ = buffer.shape
    half = count // 2
    quarter = out_refs[0].shape[1]
    piece_blocks = held_ref.shape[2] // width
    rows = [chunk_ref[number // half] * half + number % half for number in range(count)]
    copies = [
        pltpu.make_async_copy(blocks_ref.at[row], buffer.at[number], sems.at[number])
        for number, row in enumerate(rows)
    ]
    for copy in laid + copies:
        copy.start()
    for copy in laid:
        copy.wait()
    for copy in kept:
        copy.start()
    for number, row in enumerate(rows):
        copies[number].wait()
        total = None
        for slot in range(slots):
            code = code_ref[row * slots + slot]
            start = pl.multiple_of(code % piece_blocks * width, width)
            source = held_ref[code // piece_blocks, :, pl.ds(start, width)]
            term = jnp.dot(
                source, buffer[number, slot], preferred_element_type=jnp.float32
            )
            total = term if total is None else total + term
        total = total.astype(jnp.bfloat16)
        way, low = number // half, number % half * width
        for sub in range(2):
            first = max(low, sub * quarter)
            last = min(low + width, (sub + 1) * quarter)
            if first < last:
                out_refs[2 * way + sub][:, first - sub * quarter : last - sub * quarter] = (
                    total[:, first - low : last - low]
                )
    for copy in kept:
        copy.wait()


def partial_sums(chunk, code, sources, blocks, half):
    _, slots, width, _ = blocks.shape
    parts = len(sources) if isinstance(sources, list) else 0
    operands = sources if parts else [sources]
    rows = parts // 2 if parts else sources.shape[0]
    seqs, columns = sources[0].shape if parts else (sources.shape[1], sources.shape[2] // 2)
    quarter = jax.ShapeDtypeStruct((seqs, columns // 2), jnp.bfloat16)
    whole = jax.ShapeDtypeStruct((rows, seqs, 2 * columns), jnp.bfloat16)
    scratch = [
        pltpu.VMEM(whole.shape, whole.dtype),
        pltpu.VMEM((2 * half, slots, width, width), blocks.dtype),
        pltpu.SemaphoreType.DMA((2 * half,)),
        pltpu.SemaphoreType.DMA((2 * parts + 1,)),
    ]
    vmem = pl.BlockSpec(memory_space=pltpu.VMEM)
    smem = pl.BlockSpec(memory_space=pltpu.SMEM)
    anywhere = pl.BlockSpec(memory_space=pl.ANY)
    return pl.pallas_call(
        functools.partial(partial_kernel, parts),
        in_specs=[smem, smem] + [anywhere] * (len(operands) + 1),
        out_specs=[vmem] * 4 + [anywhere] * (parts > 0),
        scratch_shapes=scratch,
        out_shape=[quarter] * 4 + [whole] * (parts > 0),
        cost_estimate=pl.CostEstimate(
            flops=4 * half * slots * seqs * width * width,
            bytes_accessed=4 * half * slots * width * width + 8 * seqs * columns,
            transcendentals=0,
        ),
        compiler_params=pltpu.CompilerParams(vmem_limit_bytes=24 << 20),
        name="partial_sums",
    )(chunk, code, *operands, blocks)


def on_device(blocks, source_ids, emission, tokens):
    row_count = lax.axis_size("row")
    col_count = lax.axis_size("col")
    row_index = lax.axis_index("row")
    col_index = lax.axis_index("col")
    local_rows, local_slots, width, _ = blocks.shape
    vocab_local, panel = emission.shape
    piece = panel // col_count
    piece_blocks = piece // width
    half = piece_blocks // 2
    total_steps, seq_count = tokens.shape
    states = panel * row_count

    owner = tokens // vocab_local
    inner = tokens % vocab_local
    same = owner[:, :, None] == owner[:, None, :]
    earlier = jnp.arange(seq_count)[:, None] > jnp.arange(seq_count)[None, :]
    rank = jnp.sum((same & earlier[None]).astype(jnp.int32), axis=2)
    mine = (owner == col_index)[:, None, :] & (
        rank[:, None, :] == jnp.arange(CAP_PAD)[None, :, None]
    )
    ids = jnp.sum(jnp.where(mine, inner[:, None, :], 0), axis=2)
    index = owner * (FOLD * CAP) + rank

    def exchange(values):
        return lax.all_to_all(values, "col", 0, 0, tiled=True)

    first = jnp.take(emission, ids[0, :CAP], axis=0, mode="clip")
    sent_pairs = fold_rows(first, col_count)
    ids_later, sent_pairs = lax.optimization_barrier((ids[1:], sent_pairs))
    later = pick(ids_later, emission, col_count)
    quarter = piece // 4

    def split(whole):
        return [whole[:, n * quarter : (n + 1) * quarter] for n in range(4)]

    def gather_rows(own):
        found = {0: own}
        bit = row_count // 2
        while bit:
            pairs = [(i, i ^ bit) for i in range(row_count)]
            for key in list(found):
                found[key ^ bit] = lax.ppermute(found[key], "row", pairs)
            bit //= 2
        return [found[key] for key in range(row_count)]

    sent_b, later, index_first = lax.optimization_barrier((sent_pairs[1], later, index[0]))
    start_a = place(index_first, exchange(sent_pairs[0]))
    held_a = gather_rows(start_a)
    came_b, _ = lax.optimization_barrier((exchange(sent_b), held_a))
    start_b = place(index_first, came_b)
    held_pairs = [held_a, gather_rows(start_b)]
    ready = start_b

    group = source_ids // piece_blocks
    code = ((group // col_count) ^ row_index) * piece_blocks + source_ids % piece_blocks
    code = code.reshape(-1).astype(jnp.int32)

    order = ring_order(col_count)
    position = jnp.array([order.index(c) for c in range(col_count)], jnp.int32)[col_index]
    order_table = jnp.array(order, jnp.int32)
    hops = jnp.arange(col_count, dtype=jnp.int32)
    up = order_table[(position - 1 - hops) % col_count]
    down = order_table[(position + 1 + hops) % col_count]
    chunks = jnp.stack([2 * up, 2 * down + 1], axis=1)
    forward = [(order[i], order[(i + 1) % col_count]) for i in range(col_count)]
    backward = [(target, source) for source, target in forward]
    directions = (forward, backward)

    def add(mine, came):
        return (mine.astype(jnp.float32) + came.astype(jnp.float32)).astype(jnp.bfloat16)

    for step in range(1, total_steps):
        sent, _ = lax.optimization_barrier((later[step - 1], ready))
        came_weights = exchange(sent)
        held = [pair[key] for key in range(row_count) for pair in held_pairs]
        *value, held = partial_sums(chunks[0], code, held, blocks, half)
        for hop in range(1, col_count):
            came = [lax.ppermute(v, "col", directions[n // 2]) for n, v in enumerate(value)]
            if hop == col_count - 1:
                break
            chunk, _ = lax.optimization_barrier((chunks[hop], value[0::2]))
            if hop == 2:
                chunk, came_weights, own = lax.optimization_barrier((chunk, came_weights, own))
            value = list(partial_sums(chunk, code, held, blocks, half))
            if hop == 1:
                chunk, _ = lax.optimization_barrier((chunks[-1], value))
                own = partial_sums(chunk, code, held, blocks, half)
            value[0::2] = [add(v, c) for v, c in zip(value[0::2], came[0::2])]
            came[1::2], _ = lax.optimization_barrier((came[1::2], value[0::2]))
            value[1::2] = [add(v, c) for v, c in zip(value[1::2], came[1::2])]
        weights = split(place(index[step], came_weights))
        weighted = [None] * 4
        came[1::2], came[0::2] = lax.optimization_barrier((came[1::2], came[0::2]))
        for n in range(4):
            carried = own[n].astype(jnp.float32) + came[n].astype(jnp.float32)
            weighted[n] = carried * weights[n].astype(jnp.float32)
        if step < total_steps - 1:
            now = [w.astype(jnp.bfloat16) for w in weighted]
            now = [jnp.concatenate(now[pair::2], axis=1) for pair in range(2)]
            held_pairs = [gather_rows(pair) for pair in now]
            ready = now[1]

    total = functools.reduce(jnp.add, [jnp.sum(w, axis=1) for w in weighted])
    devices = row_count * col_count
    totals = jnp.broadcast_to(total, (devices, SUBLANES, seq_count))
    totals = lax.all_to_all(totals, ("row", "col"), 0, 0, tiled=True)
    total = jnp.sum(totals[:, 0, :], axis=0)
    scale = total / states
    posterior = jnp.concatenate([w / scale[:, None] for w in weighted], axis=1)
    return posterior.astype(jnp.bfloat16), jnp.log(scale)


def solution(mesh):
    in_specs = (P("row", "col", None, None), P("row", "col"), P("col", "row"), P())
    out_specs = (P(None, ("row", "col")), P())
    return jax.shard_map(
        on_device, mesh=mesh, in_specs=in_specs, out_specs=out_specs, check_vma=False
    )
```
